768 devices in a mesh: group: 16 (over x, z_hi, core), replica: 48 (over z_lo, y).
Axes of the slice: x: 4, y: 8, z: 12 (z_hi: 2, z_lo: 6; z = z_hi * 6 + z_lo), core: 2. Of those that a mesh axis runs over, the one named last changes fastest.
Arguments:
- grad_parts: bfloat16 [48, 48, 512, 512], P('replica', None, 'group'), may hold values from -1 to 1
- owner_order: int32 [48], replicated, may hold values from 0 to 47, each once
- step_count: int32 [1], replicated, may hold values from 1 to 12
- stat_old: float32 [48, 512, 512], P('replica'), as said below
- root_old: bfloat16 [48, 512, 512], P('replica'), may hold values from -0.25 to 0.25
Outputs:
- update: bfloat16 [48, 512, 512], P(None, 'group')
- stat_new: float32 [48, 512, 512], P('replica')
- root_new: bfloat16 [48, 512, 512], P('replica')
The draws below stay inside these ranges and needn't reach their ends.
Inputs may be any that keep to these rules, and one draw needn't show every extreme that they name: `stat_old`: each matrix is symmetric positive definite.
All inputs are finite; a program needn't handle non-finite values.
Results may differ from the reference program's by a relative error of at most 0.001.
The reference program's roundings to bfloat16 on the way count: a program that leaves them out, or rounds other values in their place, can miss the bound.
Values may be sent and summed in bfloat16 or wider, within the bound.
A program may use at most 32 MiB of HBM per device.

```python
import jax
import jax.numpy as jnp
from jax import lax

BW = 512
ITERS = 3
NBLK = 48
ROWS = 512
N_REPLICA = 48


def draw_stat_old(key, part):
    first = jax.random.fold_in(jax.random.fold_in(key, 7), 0)
    factor = jax.random.normal(first, (NBLK, BW, BW), jnp.float32)
    product = jnp.einsum('bik,bjk->bij', factor, factor)
    return product + 0.1 * ROWS * jnp.eye(BW, dtype=jnp.float32)


def spiked(entries, rng, source, target, blocks, factor):
    def block_of(axis_at):
        return (jnp.arange(entries.shape[axis_at]) // (entries.shape[axis_at] // blocks)).reshape((-1,) + (1,) * (entries.ndim - 1 - axis_at))

    near = jax.random.permutation(rng, blocks)[block_of(target)]
    other_side = (block_of(target) + blocks // 2) % blocks
    return jnp.where((block_of(source) == near) | (block_of(source) == other_side), factor * entries, entries)


def level_of(rng, dims, pieces, low, high):
    gain, own = 1.0, jax.random.fold_in(rng, 6)
    for dim, shards_of in pieces:
        draws = jnp.exp(jax.random.uniform(jax.random.fold_in(own, dim), (shards_of,), jnp.float32, low / len(pieces), high / len(pieces)))
        gain = gain * jnp.repeat(draws, dims[dim] // shards_of).reshape([-1 if axis == dim else 1 for axis in range(len(dims))])
    return gain


def scatter_about(key, shape, spread, most, cuts=(), kind=jnp.bfloat16):
    array = spread * jax.random.normal(key, shape, jnp.float32)
    if cuts:
        array = array * level_of(key, shape, cuts, -0.22, 0.18)
    return jnp.clip(array, -most, most).astype(kind)


def heavy_noise(stream_key, dims, scale, most, shards, heavy, kind=jnp.bfloat16):
    entries = scale * jax.random.normal(stream_key, dims, jnp.float32)
    if shards:
        entries = entries * level_of(stream_key, dims, shards, -0.22, 0.18)
    return jnp.clip(spiked(entries, jax.random.fold_in(stream_key, 3), *heavy), -most, most).astype(kind)


def setup_inputs(seed: int = 0) -> dict:
    keys = jax.random.split(jax.random.key(seed), 6)
    grad_parts = heavy_noise(keys[0], (N_REPLICA, NBLK, ROWS, BW), 0.15, 1.0, ((0, 48), (2, 16)), (0, 1, 48, 3.25))
    owner_order = jax.random.permutation(keys[1], NBLK).astype(jnp.int32)
    step_count = jax.random.randint(keys[2], (1,), 1, 13).astype(jnp.int32)
    stat_old = draw_stat_old(jax.random.fold_in(keys[5], 71), 0)
    root_old = scatter_about(keys[4], (NBLK, BW, BW), BW ** -0.5, 0.25, ((0, 48),))
    return dict(grad_parts=grad_parts, owner_order=owner_order, step_count=step_count, stat_old=stat_old, root_old=root_old)


decay_rate = 0.95
epsilon = 0.001

def newton(shifted):
    identity = jnp.eye(BW, dtype=jnp.float32)
    frobenius = jnp.sqrt(jnp.sum(shifted * shifted))
    coupled = shifted / frobenius
    root_iter = identity * frobenius ** (-0.25)
    for repeat in range(ITERS):
        factor = (5.0 * identity - coupled) * 0.25
        root_iter = jnp.dot(root_iter, factor, precision=lax.Precision.HIGHEST)
        if repeat + 1 < ITERS:
            factor_sq = jnp.dot(factor, factor, precision=lax.Precision.HIGHEST)
            factor_quad = jnp.dot(factor_sq, factor_sq, precision=lax.Precision.HIGHEST)
            coupled = jnp.dot(factor_quad, coupled, precision=lax.Precision.HIGHEST)
    return root_iter

def reference(grad_parts, owner_order, step_count, stat_old, root_old):

    def add_one(replica_index, running):
        return running + grad_parts[replica_index].astype(jnp.float32)
    summed = lax.fori_loop(0, N_REPLICA, add_one, jnp.zeros((NBLK, ROWS, BW), jnp.float32))
    slot_grads = summed[owner_order]
    gram_matrix = jnp.einsum('bri,brj->bij', slot_grads, slot_grads, precision=lax.Precision.HIGHEST)
    rounded = slot_grads.astype(jnp.bfloat16).astype(jnp.float32)
    products = jnp.einsum('bri,bij->brj', rounded, root_old.astype(jnp.float32))
    grad_norm = jnp.trace(gram_matrix, axis1=1, axis2=2)
    update_norm = lax.optimization_barrier(jnp.sum(products * products, axis=(1, 2)))
    graft_scale = jnp.sqrt(grad_norm / (update_norm + 1e-06))
    scaled = (graft_scale[:, None, None] * products).astype(jnp.bfloat16)
    update = jnp.zeros_like(scaled).at[owner_order].set(scaled)
    stat_new = decay_rate * stat_old + (1.0 - decay_rate) * gram_matrix
    correction = 1.0 / (1.0 - decay_rate ** step_count[0].astype(jnp.float32))
    shifted = stat_new * correction + epsilon * jnp.eye(BW, dtype=jnp.float32)
    root_new = lax.map(newton, shifted).astype(jnp.bfloat16)
    return (update, stat_new, root_new)
```

```python
import jax
import jax.numpy as jnp
from jax import lax
from jax.experimental import pallas as pl
from jax.experimental.pallas import tpu as pltpu
from jax.sharding import PartitionSpec as P

ITERS = 3
DECAY = 0.95
EPS = 0.001
NY, NZ = 8, 6
NB, ROWS, W = 48, 32, 512
CA = 384
F32, BF16 = jnp.float32, jnp.bfloat16


def split(value):
    high = value.astype(BF16)
    return high, (value - high.astype(F32)).astype(BF16)


def eye_block(first, rows):
    row = lax.broadcasted_iota(jnp.int32, (rows, W), 0) + first
    return row == lax.broadcasted_iota(jnp.int32, (rows, W), 1)


def kernel(
    order, inverse, step, gp, stat_hbm, root_hbm,
    update, stat_out, root_out,
    raw_y, raw_y_in, sum_y, sum_y_in, raw_z, raw_z_in, tot_z, tot_z_in, fin_z, fin_z_in,
    owned, norms, norms_in, rows_all, stat_v, root_v, gathered,
    th, tl, mh, ml, qh, ql, xh, xl, shifted,
    y_s, y_r, zr_s, zr_r, zt_s, zt_r, zf_s, zf_r, nb_s, nb_r, gx_s, gx_r, gc_s, gc_r, gz_s, gz_r,
    cz_s, cz_r, cy_s, cy_r, loc,
):
    g, r = lax.axis_index("group"), lax.axis_index("replica")
    x, zh, c = g // 4, lax.rem(g // 2, 2), lax.rem(g, 2)
    z, y = r // NY, lax.rem(r, NY)

    def gid(xx, hh, cc):
        return xx * 4 + hh * 2 + cc

    def yy(d):
        return lax.rem(y + d + NY, NY)

    def zz(d):
        return lax.rem(z + d, NZ)

    def at_y(d):
        return g, z * NY + yy(d)

    def at_z(k):
        return g, zz(k + 1) * NY + y

    started = []

    def describe(src, dst, ss, rs, dev):
        return pltpu.make_async_remote_copy(
            src_ref=src, dst_ref=dst, send_sem=ss, recv_sem=rs,
            device_id=dev, device_id_type=pl.DeviceIdType.MESH,
        )

    def put(src, dst, ss, rs, dev):
        copy = describe(src, dst, ss, rs, dev)
        copy.start()
        started.append(copy)

    def arrived(dst, ss, rs, dev):
        describe(dst, dst, ss, rs, dev).wait_recv()

    stat_copy = pltpu.make_async_copy(stat_hbm.at[0], stat_v, loc.at[0])
    root_copy = pltpu.make_async_copy(root_hbm.at[0], root_v, loc.at[1])
    stat_copy.start()
    root_copy.start()

    barrier = pltpu.get_barrier_semaphore()
    peers = [at_y(d) for d in range(1, NY)] + [at_z(k) for k in range(NZ - 1)]
    peers += [(lax.rem(g + m, 16), r) for m in range(1, 16)]
    for dev in peers:
        pl.semaphore_signal(barrier, inc=1, device_id=dev, device_id_type=pl.DeviceIdType.MESH)

    def block(k, d, first, width):
        return gp[0, order[zz(k + 1) * NY + yy(d)], :, pl.ds(first, width)]

    def reach(way, k):
        return 4 if (way + k) % 2 == 0 else 3

    step_of = (1, -1)
    for k in range(NZ):
        for way in range(2):
            raw_y[way, k] = block(k, step_of[way] * reach(way, k), 0, CA)
    for k in range(NZ - 1):
        for d in range(NY):
            raw_z[k, d] = block(k, d, CA, W - CA)
    pl.semaphore_wait(barrier, len(peers))

    def near(way):
        return at_y(step_of[way])

    for k in range(NZ):
        for way in range(2):
            at = reach(way, k) - 1
            put(raw_y.at[way, k], raw_y_in.at[way, k], y_s.at[way, k, at], y_r.at[way, k, at], near(way))
    for k in range(NZ - 1):
        put(raw_z.at[k], raw_z_in.at[k], zr_s.at[k], zr_r.at[k], at_z(k))

    def incoming(way, k, d):
        if d == reach(way, k):
            arrived(raw_y_in.at[way, k], y_s.at[way, k, d - 1], y_r.at[way, k, d - 1], near(way))
            return raw_y_in[way, k].astype(F32)
        arrived(sum_y_in.at[way, k, d - 1], y_s.at[way, k, d - 1], y_r.at[way, k, d - 1], near(way))
        return sum_y_in[way, k, d - 1]

    def pass_on(d):
        for k in range(NZ):
            for way in range(2):
                if d < reach(way, k):
                    total = incoming(way, k, d + 1) + block(k, step_of[way] * d, 0, CA).astype(F32)
                    sum_y[way, k, d - 1] = total
                    put(sum_y.at[way, k, d - 1], sum_y_in.at[way, k, d - 1], y_s.at[way, k, d - 1], y_r.at[way, k, d - 1], near(way))

    pass_on(3)
    pass_on(2)
    for k in range(NZ - 1):
        arrived(raw_z_in.at[k], zr_s.at[k], zr_r.at[k], at_z(k))
    for d in range(NY):
        total = block(NZ - 1, d, CA, W - CA).astype(F32)
        for k in range(NZ - 1):
            total += raw_z_in[k, d].astype(F32)
        tot_z[d] = total
        if d:
            put(tot_z.at[d], tot_z_in.at[d - 1], zt_s.at[d - 1], zt_r.at[d - 1], at_y(d))
    pass_on(1)
    for k in range(NZ):
        total = incoming(0, k, 1) + incoming(1, k, 1) + block(k, 0, 0, CA).astype(F32)
        if k < NZ - 1:
            fin_z[k] = total
            put(fin_z.at[k], fin_z_in.at[k], zf_s.at[k], zf_r.at[k], at_z(k))
        else:
            mine = total
    for k in range(NZ - 1):
        arrived(fin_z_in.at[k], zf_s.at[k], zf_r.at[k], at_z(k))
        mine += fin_z_in[k]
    owned[:, 0:CA] = mine
    mine = tot_z[0]
    for d in range(NY - 1):
        arrived(tot_z_in.at[d], zt_s.at[d], zt_r.at[d], at_y(1))
        mine += tot_z_in[d]
    owned[:, CA:W] = mine

    root_copy.wait()
    products = jnp.dot(owned[...].astype(BF16), root_v[...], preferred_element_type=F32)
    mine = owned[...]
    grad_norm = jnp.sum(jnp.sum(mine * mine, axis=1, keepdims=True), axis=0, keepdims=True)
    update_norm = jnp.sum(jnp.sum(products * products, axis=1, keepdims=True), axis=0, keepdims=True)
    upper = lax.broadcasted_iota(jnp.int32, (8, 128), 0) < 4
    norms[...] = jnp.where(upper, grad_norm, update_norm)
    for m in range(1, 16):
        put(norms, norms_in.at[m - 1], nb_s.at[m - 1], nb_r.at[m - 1], (lax.rem(g + m, 16), r))

    rows_all[g] = mine

    def xat(m):
        return lax.rem(x + m, 4)

    far, sib = gid(x, 1 - zh, c), gid(x, zh, 1 - c)
    put(rows_all.at[g], rows_all.at[g], gz_s, gz_r, (far, r))
    for m in (1, 3, 2):
        put(rows_all.at[g], rows_all.at[g], gx_s.at[0, m], gx_r.at[0, m], (gid(xat(m), zh, c), r))
    put(rows_all.at[g], rows_all.at[g], gc_s.at[0, 0], gc_r.at[0, 0], (sib, r))

    total = norms[...]
    for m in range(15):
        arrived(norms_in.at[m], nb_s.at[m], nb_r.at[m], (sib, r))
        total += norms_in[m]
    graft = jnp.sqrt(total[0:1, 0:1] / (total[4:5, 0:1] + 1e-06))
    own_slot = z * NY + y
    gathered[own_slot] = (graft * products).astype(BF16)

    for k in range(NZ - 1):
        put(gathered.at[own_slot], gathered.at[own_slot], cz_s.at[k], cz_r.at[k], at_z(k))

    def from_z(k):
        return gathered.at[lax.rem(z + NZ - 1 - k, NZ) * NY + y]

    def slot_from(k, way, hops):
        zs = z if k == NZ - 1 else lax.rem(z + NZ - 1 - k, NZ)
        return gathered.at[zs * NY + yy(-step_of[way] * hops)]

    def hop(k, h):
        for way in range(2):
            if 0 < h <= reach(way, k):
                arrived(slot_from(k, way, h), cy_s.at[way, k, h - 1], cy_r.at[way, k, h - 1], near(way))
            if h < reach(way, k):
                ref = slot_from(k, way, h)
                put(ref, ref, cy_s.at[way, k, h], cy_r.at[way, k, h], near(way))

    def first(k):
        if k < NZ - 1:
            arrived(from_z(k), cz_s.at[k], cz_r.at[k], at_z(k))
        hop(k, 0)

    first(5)
    arrived(rows_all.at[far], gz_s, gz_r, (far, r))
    for m in (1, 3, 2):
        put(rows_all.at[far], rows_all.at[far], gx_s.at[1, m], gx_r.at[1, m], (gid(xat(m), zh, c), r))
    put(rows_all.at[far], rows_all.at[far], gc_s.at[1, 0], gc_r.at[1, 0], (sib, r))
    first(0)
    first(4)
    first(1)
    first(3)
    first(2)
    for h in range(1, 5):
        for k in (5, 0, 4, 1, 3, 2):
            hop(k, h)

    for half in range(2):
        hh = zh if half == 0 else 1 - zh
        for m in (1, 3, 2):
            slot = gid(lax.rem(x + 4 - m, 4), hh, c)
            arrived(rows_all.at[slot], gx_s.at[half, m], gx_r.at[half, m], (sib, r))
            put(rows_all.at[slot], rows_all.at[slot], gc_s.at[half, m], gc_r.at[half, m], (sib, r))

    def permute(b, carry):
        update[b] = gathered[inverse[b]]
        return carry

    lax.fori_loop(0, NB, permute, 0)

    for half in range(2):
        hh = zh if half == 0 else 1 - zh
        for m in range(4):
            slot = gid(lax.rem(x + 4 - m, 4), hh, 1 - c)
            arrived(rows_all.at[slot], gc_s.at[half, m], gc_r.at[half, m], (sib, r))

    high, low = split(rows_all[...].reshape(16 * ROWS, W))
    th[...] = high
    tl[...] = low

    def rows_dot(a, b):
        return lax.dot_general(a, b, (((0,), (0,)), ((), ())), preferred_element_type=F32)

    gram = rows_dot(th[...], th[...]) + rows_dot(th[...], tl[...]) + rows_dot(tl[...], th[...])
    stat_copy.wait()
    stat_new = DECAY * stat_v[...] + (1.0 - DECAY) * gram
    stat_out[0] = stat_new
    count = step[0]
    power = jnp.float32(1.0)
    for n in range(12):
        power = jnp.where(n < count, power * DECAY, power)
    correction = 1.0 / (1.0 - jnp.full((8, 128), power, F32))
    value = stat_new * correction[0:1, 0:1] + jnp.where(eye_block(0, W), EPS, 0.0)
    shifted[...] = value
    square = jnp.sum(jnp.sum(value * value, axis=1, keepdims=True), axis=0, keepdims=True)
    frobenius = jnp.sqrt(square)
    scale = 1.0 / jnp.sqrt(jnp.sqrt(frobenius))

    half_rows = W // 2

    def factor_of(i, coupled):
        rows = pl.ds(i * half_rows, half_rows)
        mh[rows], ml[rows] = split(coupled)
        factor = (jnp.where(eye_block(i * half_rows, half_rows), 5.0, 0.0) - coupled) * 0.25
        return rows, factor

    def product(a_high, a_low, b_high, b_low, give):
        for i in range(2):
            rows = pl.ds(i * half_rows, half_rows)
            out = jnp.dot(a_high[rows], b_high[...], preferred_element_type=F32)
            out += jnp.dot(a_high[rows], b_low[...], preferred_element_type=F32)
            out += jnp.dot(a_low[rows], b_high[...], preferred_element_type=F32)
            give(i, rows, out)

    def keep(high_ref, low_ref):
        def give(i, rows, out):
            high_ref[rows], low_ref[rows] = split(out)
        return give

    for i in range(2):
        rows, factor = factor_of(i, shifted[pl.ds(i * half_rows, half_rows)] / frobenius)
        th[rows], tl[rows] = split(factor)
        xh[rows], xl[rows] = th[rows], tl[rows]
    for repeat in range(ITERS):
        if repeat:
            if repeat + 1 < ITERS:
                product(xh, xl, th, tl, keep(qh, ql))
                xh[...], xl[...] = qh[...], ql[...]
            else:
                def finish(i, rows, out):
                    root_out[0, rows] = (out * scale).astype(BF16)
                product(xh, xl, th, tl, finish)
        if repeat + 1 < ITERS:
            product(th, tl, th, tl, keep(qh, ql))
            product(qh, ql, qh, ql, keep(th, tl))

            def couple(i, rows, out):
                shifted[rows] = out
            product(th, tl, mh, ml, couple)
            for i in range(2):
                rows, factor = factor_of(i, shifted[pl.ds(i * half_rows, half_rows)])
                th[rows], tl[rows] = split(factor)

    for copy in started:
        copy.wait_send()


def local(grad_parts, owner_order, step_count, stat_old, root_old):
    slots = jnp.arange(NB, dtype=jnp.int32)
    inverse = jnp.sum(jnp.where(owner_order[None, :] == slots[:, None], slots[None, :], 0), axis=1)
    smem = pl.BlockSpec(memory_space=pltpu.SMEM)
    vmem = pl.BlockSpec(memory_space=pltpu.VMEM)
    hbm = pl.BlockSpec(memory_space=pl.ANY)
    sem = pltpu.SemaphoreType.DMA
    square = pltpu.VMEM((W, W), BF16)
    return pl.pallas_call(
        kernel,
        out_shape=(
            jax.ShapeDtypeStruct((NB, ROWS, W), BF16),
            jax.ShapeDtypeStruct((1, W, W), F32),
            jax.ShapeDtypeStruct((1, W, W), BF16),
        ),
        in_specs=[smem, smem, smem, vmem, hbm, hbm],
        out_specs=(vmem, vmem, vmem),
        scratch_shapes=[
            pltpu.VMEM((2, NZ, ROWS, CA), BF16),
            pltpu.VMEM((2, NZ, ROWS, CA), BF16),
            pltpu.VMEM((2, NZ, 3, ROWS, CA), F32),
            pltpu.VMEM((2, NZ, 3, ROWS, CA), F32),
            pltpu.VMEM((NZ - 1, NY, ROWS, W - CA), BF16),
            pltpu.VMEM((NZ - 1, NY, ROWS, W - CA), BF16),
            pltpu.VMEM((NY, ROWS, W - CA), F32),
            pltpu.VMEM((NY - 1, ROWS, W - CA), F32),
            pltpu.VMEM((NZ - 1, ROWS, CA), F32),
            pltpu.VMEM((NZ - 1, ROWS, CA), F32),
            pltpu.VMEM((ROWS, W), F32),
            pltpu.VMEM((8, 128), F32),
            pltpu.VMEM((15, 8, 128), F32),
            pltpu.VMEM((16, ROWS, W), F32),
            pltpu.VMEM((W, W), F32),
            pltpu.VMEM((W, W), BF16),
            pltpu.VMEM((NB, ROWS, W), BF16),
            square, square, square, square, square, square, square, square,
            pltpu.VMEM((W, W), F32),
            sem((2, NZ, 4)), sem((2, NZ, 4)),
            sem((NZ - 1,)), sem((NZ - 1,)),
            sem((NY - 1,)), sem((NY - 1,)),
            sem((NZ - 1,)), sem((NZ - 1,)),
            sem((15,)), sem((15,)),
            sem((2, 4)), sem((2, 4)),
            sem((2, 4)), sem((2, 4)),
            sem, sem,
            sem((NZ - 1,)), sem((NZ - 1,)),
            sem((2, NZ, 4)), sem((2, NZ, 4)),
            sem((2,)),
        ],
        compiler_params=pltpu.CompilerParams(
            collective_id=0, has_side_effects=True, vmem_limit_bytes=48 * 2**20
        ),
        name="shampoo_step",
    )(owner_order, inverse, step_count, grad_parts, stat_old, root_old)


def solution(mesh):
    placed = (
        P("replica", None, "group", None),
        P(),
        P(),
        P("replica", None, None),
        P("replica", None, None),
    )
    return jax.shard_map(
        local,
        mesh=mesh,
        in_specs=placed,
        out_specs=(P(None, "group", None), P("replica", None, None), P("replica", None, None)),
        check_vma=False,
    )
```

```python
import jax
import jax.numpy as jnp
from jax import lax
from jax.experimental import pallas as pl
from jax.experimental.pallas import tpu as pltpu
from jax.sharding import PartitionSpec as P

ITERS = 3
DECAY = 0.95
EPS = 0.001
NY, NZ = 8, 6
NB, ROWS, W = 48, 32, 512
SPLIT_K = 3
NORM_ORDER = (10, 11, 14, 15, 2, 3, 6, 7, 8, 9, 12, 13, 4, 5, 1)
AT_ACROSS, AT_FAR, AT_ACROSS_FAR, AT_WORK = 2, 8, 20, 24
CA = 384
F32, BF16 = jnp.float32, jnp.bfloat16


def split(value):
    high = value.astype(BF16)
    return high, (value - high.astype(F32)).astype(BF16)


def eye_block(first, rows):
    row = lax.broadcasted_iota(jnp.int32, (rows, W), 0) + first
    return row == lax.broadcasted_iota(jnp.int32, (rows, W), 1)


FAR = ((5, 4, 3, 2, 1, 0), (5, 4, 3, 0, 2, 1), (5, 0, 4, 1, 3, 2), (0, 5, 1, 4, 2, 3), (0, 1, 2, 5, 3, 4), (0, 1, 2, 3, 4, 5))
RING = (
    (0, 5, 0), (1, 5, 0), (0, 4, 0), (1, 4, 0), (0, 3, 0), (1, 3, 0), (0, 2, 0), (1, 2, 0), (0, 5, 1), (1, 5, 1),
    (0, 1, 0), (1, 1, 0), (0, 0, 0), (1, 0, 0), (0, 4, 1), (1, 3, 1), (0, 2, 1), (1, 2, 1), (0, 3, 1), (1, 4, 1),
    (0, 1, 1), (1, 1, 1), (0, 0, 1), (1, 0, 1), (0, 4, 2), (1, 3, 2), (1, 5, 2), (0, 2, 2), (1, 2, 2), (0, 3, 2),
    (0, 1, 2), (1, 1, 2), (0, 0, 2), (1, 0, 2), (0, 4, 3), (1, 3, 3), (0, 2, 3), (1, 4, 2), (0, 5, 2), (1, 5, 3),
    (1, 1, 3), (0, 0, 3),
)


def kernel(
    step, order_hbm, gp_hbm, stat_hbm, root_hbm,
    gathered, stat_out, root_out,
    order, gp,
    raw_y, raw_y_in, sum_y, sum_y_in, raw_z, raw_z_in, tot_z, tot_z_in, fin_z, fin_z_in,
    owned, norms, norms_in, rows_all, stat_v, root_v,
    th, tl, mh, ml, qh, ql, xh, xl, shifted,
    y_s, y_r, zr_s, zr_r, zt_s, zt_r, zf_s, zf_r, nb_s, nb_r, gx_s, gx_r, gc_s, gc_r, gz_s, gz_r,
    cz_s, cz_r, cy_s, cy_r, loc,
):
    gp_copy = pltpu.make_async_copy(gp_hbm.at[0], gp, loc.at[2])
    order_copy = pltpu.make_async_copy(order_hbm, order, loc.at[3])
    order_copy.start()
    gp_copy.start()
    g, r = lax.axis_index("group"), lax.axis_index("replica")
    x, zh, c = g // 4, lax.rem(g // 2, 2), lax.rem(g, 2)
    z, y = r // NY, lax.rem(r, NY)
    is_z = [(NZ - lax.rem(z + NZ - v, NZ)) // NZ for v in range(NZ)]
    row = [sum(FAR[v][k] * is_z[v] for v in range(NZ)) for k in range(NZ - 1)] + [z]

    def gid(xx, hh, cc):
        return xx * 4 + hh * 2 + cc

    def yy(d):
        return lax.rem(y + d + NY, NY)

    def at_y(d):
        return g, z * NY + yy(d)

    def at_z(k):
        return g, row[k] * NY + y

    started = []

    def describe(src, dst, ss, rs, dev):
        return pltpu.make_async_remote_copy(
            src_ref=src, dst_ref=dst, send_sem=ss, recv_sem=rs,
            device_id=dev, device_id_type=pl.DeviceIdType.MESH,
        )

    def put(src, dst, ss, rs, dev):
        copy = describe(src, dst, ss, rs, dev)
        copy.start()
        started.append(copy)

    def arrived(dst, ss, rs, dev):
        describe(dst, dst, ss, rs, dev).wait_recv()

    stat_copy = pltpu.make_async_copy(stat_hbm.at[0], stat_v, loc.at[0])
    root_copy = pltpu.make_async_copy(root_hbm.at[0], root_v, loc.at[1])
    barrier = pltpu.get_barrier_semaphore()
    peers = [at_y(d) for d in range(1, NY)] + [at_z(k) for k in range(NZ - 1)]
    peers += [(lax.bitwise_xor(g, m), r) for m in range(1, 16)]
    for dev in peers:
        pl.semaphore_signal(barrier, inc=1, device_id=dev, device_id_type=pl.DeviceIdType.MESH)
    stat_copy.start()
    root_copy.start()
    order_copy.wait()
    gp_copy.wait()

    def block(k, d, first, width):
        return gp[order[row[k] * NY + yy(d)], :, pl.ds(first, width)]

    def reach(way, k):
        return 4 if (way + k) % 2 == 0 else 3

    step_of = (1, -1)
    for k in range(NZ):
        for way in range(2):
            raw_y[way, k] = block(k, step_of[way] * reach(way, k), 0, CA)
    for k in range(NZ - 1):
        for d in range(NY):
            raw_z[k, d] = block(k, d, CA, W - CA)
    pl.semaphore_wait(barrier, len(peers))

    def near(way):
        return at_y(step_of[way])

    for k in range(NZ):
        for way in range(2):
            at = reach(way, k) - 1
            put(raw_y.at[way, k], raw_y_in.at[way, k], y_s.at[way, k, at], y_r.at[way, k, at], near(way))
    for k in range(NZ - 1):
        put(raw_z.at[k], raw_z_in.at[z], zr_s.at[k], zr_r.at[z], at_z(k))

    def incoming(way, k, d):
        if d == reach(way, k):
            arrived(raw_y_in.at[way, k], y_s.at[way, k, d - 1], y_r.at[way, k, d - 1], near(way))
            return raw_y_in[way, k].astype(F32)
        arrived(sum_y_in.at[way, k, d - 1], y_s.at[way, k, d - 1], y_r.at[way, k, d - 1], near(way))
        return sum_y_in[way, k, d - 1]

    def pass_on(d, ks=range(NZ)):
        for k in ks:
            for way in range(2):
                if d < reach(way, k):
                    total = incoming(way, k, d + 1) + block(k, step_of[way] * d, 0, CA).astype(F32)
                    sum_y[way, k, d - 1] = total
                    put(sum_y.at[way, k, d - 1], sum_y_in.at[way, k, d - 1], y_s.at[way, k, d - 1], y_r.at[way, k, d - 1], near(way))

    def totals():
        for k in range(NZ - 2, -1, -1):
            arrived(raw_z_in.at[row[k]], zr_s.at[k], zr_r.at[row[k]], at_z(k))
        for d in (4, 3, 5, 2, 6, 1, 7, 0):
            total = block(NZ - 1, d, CA, W - CA).astype(F32)
            for k in range(NZ - 1):
                total += raw_z_in[row[k], d].astype(F32)
            tot_z[d] = total
            if d:
                put(tot_z.at[d], tot_z_in.at[d - 1], zt_s.at[d - 1], zt_r.at[d - 1], at_y(d))

    pass_on(3)
    pass_on(2)
    pass_on(1, range(SPLIT_K))
    totals()
    pass_on(1, range(SPLIT_K, NZ))
    for k in range(NZ):
        total = incoming(0, k, 1) + incoming(1, k, 1) + block(k, 0, 0, CA).astype(F32)
        if k < NZ - 1:
            fin_z[k] = total
            put(fin_z.at[k], fin_z_in.at[z], zf_s.at[k], zf_r.at[z], at_z(k))
        else:
            owned[:, 0:CA] = total
    mine = tot_z[0]
    for d in range(NY - 1):
        arrived(tot_z_in.at[d], zt_s.at[d], zt_r.at[d], at_y(1))
        mine += tot_z_in[d]
    owned[:, CA:W] = mine
    mine = owned[:, 0:CA]
    for k in range(NZ - 1):
        arrived(fin_z_in.at[row[k]], zf_s.at[k], zf_r.at[row[k]], at_z(k))
        mine += fin_z_in[row[k]]
    owned[:, 0:CA] = mine

    root_copy.wait()
    products = jnp.dot(owned[...].astype(BF16), root_v[...], preferred_element_type=F32)
    mine = owned[...]
    grad_norm = jnp.sum(jnp.sum(mine * mine, axis=1, keepdims=True), axis=0, keepdims=True)
    update_norm = jnp.sum(jnp.sum(products * products, axis=1, keepdims=True), axis=0, keepdims=True)
    upper = lax.broadcasted_iota(jnp.int32, (8, 128), 0) < 4
    norms[...] = jnp.where(upper, grad_norm, update_norm)
    for m in NORM_ORDER:
        put(norms, norms_in.at[m - 1], nb_s.at[m - 1], nb_r.at[m - 1], (lax.bitwise_xor(g, m), r))

    rows_all[g] = mine

    def xat(m):
        return lax.rem(x + m, 4)

    far, sib = gid(x, 1 - zh, c), gid(x, zh, 1 - c)
    put(rows_all.at[g], rows_all.at[g], gz_s, gz_r, (far, r))
    for m in (1, 3, 2):
        put(rows_all.at[g], rows_all.at[g], gx_s.at[0, m], gx_r.at[0, m], (gid(xat(m), zh, c), r))
    put(rows_all.at[g], rows_all.at[g], gc_s.at[0, 0], gc_r.at[0, 0], (sib, r))

    total = norms[...]
    for m in range(15):
        arrived(norms_in.at[m], nb_s.at[m], nb_r.at[m], (sib, r))
        total += norms_in[m]
    graft = jnp.sqrt(total[0:1, 0:1] / (total[4:5, 0:1] + 1e-06))
    own_slot = z * NY + y
    gathered[own_slot] = (graft * products).astype(BF16)

    for k in range(NZ - 1):
        put(gathered.at[own_slot], gathered.at[own_slot], cz_s.at[k], cz_r.at[z], at_z(k))

    def slot_from(k, way, hops):
        return gathered.at[row[k] * NY + yy(-step_of[way] * hops)]

    def hop(way, k, h):
        ref = slot_from(k, way, h)
        if h:
            arrived(ref, cy_s.at[way, k, h - 1], cy_r.at[way, k, h - 1], near(way))
        elif way == 0 and k < NZ - 1:
            arrived(gathered.at[row[k] * NY + y], cz_s.at[k], cz_r.at[row[k]], at_z(k))
        if h < reach(way, k):
            put(ref, ref, cy_s.at[way, k, h], cy_r.at[way, k, h], near(way))

    def rows_from(half, m, cc):
        hh = zh if half == 0 else 1 - zh
        return rows_all.at[gid(lax.rem(x + 4 - m, 4), hh, cc)]

    def across(half):
        def go():
            for m in (1, 3, 2):
                ref = rows_from(half, m, c)
                arrived(ref, gx_s.at[half, m], gx_r.at[half, m], (sib, r))
                put(ref, ref, gc_s.at[half, m], gc_r.at[half, m], (sib, r))
        return go

    def far_rows():
        ref = rows_all.at[far]
        arrived(ref, gz_s, gz_r, (far, r))
        for m in (1, 3, 2):
            put(ref, ref, gx_s.at[1, m], gx_r.at[1, m], (gid(xat(m), zh, c), r))
        put(ref, ref, gc_s.at[1, 0], gc_r.at[1, 0], (sib, r))

    def all_rows():
        stat_copy.wait()
        for half in range(2):
            for m in range(4):
                arrived(rows_from(half, m, 1 - c), gc_s.at[half, m], gc_r.at[half, m], (sib, r))
        th[...], tl[...] = split(rows_all[...].reshape(16 * ROWS, W))

    half_rows = W // 2
    halves = [pl.ds(i * half_rows, half_rows) for i in range(2)]

    def rows_dot(a, b):
        return lax.dot_general(a, b, (((0,), (0,)), ((), ())), preferred_element_type=F32)

    def statistic(i):
        def go():
            rows = halves[i]
            gram = rows_dot(th[:, rows], th[...]) + rows_dot(th[:, rows], tl[...]) + rows_dot(tl[:, rows], th[...])
            stat_new = DECAY * stat_v[rows] + (1.0 - DECAY) * gram
            stat_out[0, rows] = stat_new
            count = step[0]
            power = jnp.float32(1.0)
            for n in range(12):
                power = jnp.where(n < count, power * DECAY, power)
            correction = 1.0 / (1.0 - jnp.full((8, 128), power, F32))
            shifted[rows] = stat_new * correction[0:1, 0:1] + jnp.where(eye_block(i * half_rows, half_rows), EPS, 0.0)
        return go

    def frobenius():
        value = shifted[...]
        return jnp.sqrt(jnp.sum(jnp.sum(value * value, axis=1, keepdims=True), axis=0, keepdims=True))

    def factor_from(i, coupled):
        rows = halves[i]
        mh[rows], ml[rows] = split(coupled)
        th[rows], tl[rows] = split((jnp.where(eye_block(i * half_rows, half_rows), 5.0, 0.0) - coupled) * 0.25)

    norm_of = []

    def start_newton():
        norm_of.append(frobenius())
        for i in range(2):
            factor_from(i, shifted[halves[i]] / norm_of[0])
            xh[halves[i]], xl[halves[i]] = th[halves[i]], tl[halves[i]]

    def product(a_high, a_low, b_high, b_low, give):
        def piece(i):
            def go():
                rows = halves[i]
                out = jnp.dot(a_high[rows], b_high[...], preferred_element_type=F32)
                out += jnp.dot(a_high[rows], b_low[...], preferred_element_type=F32)
                out += jnp.dot(a_low[rows], b_high[...], preferred_element_type=F32)
                give(i, rows, out)
            return go
        return [piece(0), piece(1)]

    def keep(high_ref, low_ref):
        def give(i, rows, out):
            high_ref[rows], low_ref[rows] = split(out)
        return give

    def couple(i, rows, out):
        shifted[rows] = out

    def next_factor():
        for i in range(2):
            factor_from(i, shifted[halves[i]])

    def take_x():
        xh[...], xl[...] = qh[...], ql[...]

    def finish(i, rows, out):
        root_out[0, rows] = (out / jnp.sqrt(jnp.sqrt(norm_of[0]))).astype(BF16)

    work = [all_rows, statistic(0), statistic(1), start_newton]
    for repeat in range(ITERS):
        last = repeat + 1 == ITERS
        if repeat:
            work += product(xh, xl, th, tl, finish if last else keep(qh, ql))
            if not last:
                work.append(take_x)
        if not last:
            work += product(th, tl, th, tl, keep(qh, ql))
            work += product(qh, ql, qh, ql, keep(th, tl))
            work += product(th, tl, mh, ml, couple)
            work.append(next_factor)

    ends = [(way, k, reach(way, k)) for k in (3, 2, 4, 5, 1, 0) for way in range(2)]
    for place, (way, k, h) in enumerate(RING + tuple(ends)):
        if place == AT_ACROSS:
            across(0)()
        if place == AT_FAR:
            far_rows()
        if place == AT_ACROSS_FAR:
            across(1)()
        if place >= AT_WORK and work:
            work.pop(0)()
        hop(way, k, h)
    for piece in work:
        piece()

    for copy in started:
        copy.wait_send()


def place_kernel(order, slots, stat, root, update, stat_out, root_out, sems):
    def update_copy(j):
        return pltpu.make_async_copy(slots.at[j], update.at[order[j]], sems.at[j])

    others = [
        pltpu.make_async_copy(stat, stat_out, sems.at[NB]),
        pltpu.make_async_copy(root, root_out, sems.at[NB + 1]),
    ]
    for copy in others:
        copy.start()
    for j in range(NB):
        update_copy(j).start()
    for copy in others:
        copy.wait()
    for j in range(NB):
        update_copy(j).wait()


def local(grad_parts, owner_order, step_count, stat_old, root_old):
    smem = pl.BlockSpec(memory_space=pltpu.SMEM)
    vmem = pl.BlockSpec(memory_space=pltpu.VMEM)
    hbm = pl.BlockSpec(memory_space=pltpu.HBM)
    sem = pltpu.SemaphoreType.DMA
    square = pltpu.VMEM((W, W), BF16)
    shapes = (
        jax.ShapeDtypeStruct((NB, ROWS, W), BF16),
        jax.ShapeDtypeStruct((1, W, W), F32),
        jax.ShapeDtypeStruct((1, W, W), BF16),
    )
    slots, stat_new, root_new = pl.pallas_call(
        kernel,
        out_shape=shapes,
        in_specs=[smem, hbm, hbm, hbm, hbm],
        out_specs=(vmem, vmem, vmem),
        scratch_shapes=[
            pltpu.SMEM((NB,), jnp.int32),
            pltpu.VMEM((NB, ROWS, W), BF16),
            pltpu.VMEM((2, NZ, ROWS, CA), BF16),
            pltpu.VMEM((2, NZ, ROWS, CA), BF16),
            pltpu.VMEM((2, NZ, 3, ROWS, CA), F32),
            pltpu.VMEM((2, NZ, 3, ROWS, CA), F32),
            pltpu.VMEM((NZ - 1, NY, ROWS, W - CA), BF16),
            pltpu.VMEM((NZ, NY, ROWS, W - CA), BF16),
            pltpu.VMEM((NY, ROWS, W - CA), F32),
            pltpu.VMEM((NY - 1, ROWS, W - CA), F32),
            pltpu.VMEM((NZ - 1, ROWS, CA), F32),
            pltpu.VMEM((NZ, ROWS, CA), F32),
            pltpu.VMEM((ROWS, W), F32),
            pltpu.VMEM((8, 128), F32),
            pltpu.VMEM((15, 8, 128), F32),
            pltpu.VMEM((16, ROWS, W), F32),
            pltpu.VMEM((W, W), F32),
            pltpu.VMEM((W, W), BF16),
            square, square, square, square, square, square, square, square,
            pltpu.VMEM((W, W), F32),
            sem((2, NZ, 4)), sem((2, NZ, 4)),
            sem((NZ - 1,)), sem((NZ,)),
            sem((NY - 1,)), sem((NY - 1,)),
            sem((NZ - 1,)), sem((NZ,)),
            sem((15,)), sem((15,)),
            sem((2, 4)), sem((2, 4)),
            sem((2, 4)), sem((2, 4)),
            sem, sem,
            sem((NZ - 1,)), sem((NZ,)),
            sem((2, NZ, 4)), sem((2, NZ, 4)),
            sem((4,)),
        ],
        compiler_params=pltpu.CompilerParams(
            collective_id=0, has_side_effects=True, vmem_limit_bytes=48 * 2**20
        ),
        name="shampoo_step",
    )(step_count, *(pltpu.with_memory_space_constraint(a, pltpu.HBM) for a in (owner_order, grad_parts, stat_old, root_old)))
    return pl.pallas_call(
        place_kernel,
        out_shape=shapes,
        in_specs=[smem, vmem, vmem, vmem],
        out_specs=(hbm, hbm, hbm),
        scratch_shapes=[sem((NB + 2,))],
        compiler_params=pltpu.CompilerParams(vmem_limit_bytes=8 * 2**20),
        name="place",
    )(owner_order, slots, stat_new, root_new)


def solution(mesh):
    placed = (
        P("replica", None, "group", None),
        P(),
        P(),
        P("replica", None, None),
        P("replica", None, None),
    )
    return jax.shard_map(
        local,
        mesh=mesh,
        in_specs=placed,
        out_specs=(P(None, "group", None), P("replica", None, None), P("replica", None, None)),
        check_vma=False,
    )
```

```python
import jax
import jax.numpy as jnp
from jax import lax
from jax.experimental import pallas as pl
from jax.experimental.pallas import tpu as pltpu
from jax.sharding import PartitionSpec as P

ITERS = 3
DECAY = 0.95
EPS = 0.001
NY, NZ = 8, 6
NB, ROWS, W = 48, 32, 512
NORM_ORDER = (10, 11, 14, 15, 2, 3, 6, 7, 8, 9, 12, 13, 4, 5, 1)
AT_ACROSS, AT_FAR, AT_ACROSS_FAR, AT_WORK = 2, 10, 22, 26
CA = 384
F32, BF16 = jnp.float32, jnp.bfloat16


def split(value):
    high = value.astype(BF16)
    return high, (value - high.astype(F32)).astype(BF16)


def eye_block(first, rows):
    row = lax.broadcasted_iota(jnp.int32, (rows, W), 0) + first
    return row == lax.broadcasted_iota(jnp.int32, (rows, W), 1)


FAR = ((5, 4, 3, 2, 1, 0), (5, 4, 3, 0, 2, 1), (5, 0, 4, 1, 3, 2), (0, 5, 1, 4, 2, 3), (0, 1, 2, 5, 3, 4), (0, 1, 2, 3, 4, 5))
RING = (
    (0, 5, 0), (1, 5, 0), (0, 4, 0), (1, 4, 0), (0, 3, 0), (1, 3, 0), (0, 2, 0), (1, 2, 0), (0, 5, 1), (1, 5, 1),
    (0, 1, 0), (1, 1, 0), (0, 0, 0), (1, 0, 0), (0, 4, 1), (1, 3, 1), (0, 2, 1), (1, 2, 1), (0, 3, 1), (1, 4, 1),
    (0, 1, 1), (1, 1, 1), (0, 0, 1), (1, 0, 1), (0, 4, 2), (1, 3, 2), (1, 5, 2), (0, 2, 2), (1, 2, 2), (0, 3, 2),
    (0, 1, 2), (1, 1, 2), (0, 0, 2), (1, 0, 2), (0, 4, 3), (1, 3, 3), (0, 2, 3), (1, 4, 2), (0, 5, 2), (1, 5, 3),
    (1, 1, 3), (0, 0, 3),
)


def kernel(
    step, order_hbm, gp_hbm, stat_hbm, root_hbm,
    gathered, stat_out, root_out,
    order, gp,
    raw_y, raw_y_in, sum_y, sum_y_in, raw_z, raw_z_in, tot_z, tot_z_in, fin_z, fin_z_in,
    owned, norms, norms_in, rows_all, stat_v, root_v,
    th, tl, mh, ml, qh, ql, xh, xl, shifted,
    y_s, y_r, zr_s, zr_r, zt_s, zt_r, zf_s, zf_r, nb_s, nb_r, gx_s, gx_r, gc_s, gc_r, gz_s, gz_r,
    cz_s, cz_r, cy_s, cy_r, loc,
):
    gp_copy = pltpu.make_async_copy(gp_hbm.at[0], gp, loc.at[2])
    order_copy = pltpu.make_async_copy(order_hbm, order, loc.at[3])
    order_copy.start()
    gp_copy.start()
    g, r = lax.axis_index("group"), lax.axis_index("replica")
    x, zh, c = g // 4, lax.rem(g // 2, 2), lax.rem(g, 2)
    z, y = r // NY, lax.rem(r, NY)
    is_z = [(NZ - lax.rem(z + NZ - v, NZ)) // NZ for v in range(NZ)]
    row = [sum(FAR[v][k] * is_z[v] for v in range(NZ)) for k in range(NZ - 1)] + [z]

    def gid(xx, hh, cc):
        return xx * 4 + hh * 2 + cc

    def yy(d):
        return lax.rem(y + d + NY, NY)

    def at_y(d):
        return g, z * NY + yy(d)

    def at_z(k):
        return g, row[k] * NY + y

    started = []

    def describe(src, dst, ss, rs, dev):
        return pltpu.make_async_remote_copy(
            src_ref=src, dst_ref=dst, send_sem=ss, recv_sem=rs,
            device_id=dev, device_id_type=pl.DeviceIdType.MESH,
        )

    def put(src, dst, ss, rs, dev):
        copy = describe(src, dst, ss, rs, dev)
        copy.start()
        started.append(copy)

    def arrived(dst, ss, rs, dev):
        describe(dst, dst, ss, rs, dev).wait_recv()

    stat_copy = pltpu.make_async_copy(stat_hbm.at[0], stat_v, loc.at[0])
    root_copy = pltpu.make_async_copy(root_hbm.at[0], root_v, loc.at[1])
    barrier = pltpu.get_barrier_semaphore()
    peers = [at_y(d) for d in range(1, NY)] + [at_z(k) for k in range(NZ - 1)]
    peers += [(lax.bitwise_xor(g, m), r) for m in range(1, 16)]
    for dev in peers:
        pl.semaphore_signal(barrier, inc=1, device_id=dev, device_id_type=pl.DeviceIdType.MESH)
    stat_copy.start()
    root_copy.start()
    order_copy.wait()
    gp_copy.wait()

    def block(k, d, first, width):
        return gp[order[row[k] * NY + yy(d)], :, pl.ds(first, width)]

    def reach(way, k):
        return 4 if (way + k) % 2 == 0 else 3

    step_of = (1, -1)
    for k in range(NZ):
        for way in range(2):
            raw_y[way, k] = block(k, step_of[way] * reach(way, k), 0, CA)
    for k in range(NZ - 1):
        for d in range(NY):
            raw_z[k, d] = block(k, d, CA, W - CA)
    pl.semaphore_wait(barrier, len(peers))

    def near(way):
        return at_y(step_of[way])

    for k in range(NZ):
        for way in range(2):
            at = reach(way, k) - 1
            put(raw_y.at[way, k], raw_y_in.at[way, k], y_s.at[way, k, at], y_r.at[way, k, at], near(way))
    for k in range(NZ - 1):
        put(raw_z.at[k], raw_z_in.at[z], zr_s.at[k], zr_r.at[z], at_z(k))

    def incoming(way, k, d):
        if d == reach(way, k):
            arrived(raw_y_in.at[way, k], y_s.at[way, k, d - 1], y_r.at[way, k, d - 1], near(way))
            return raw_y_in[way, k].astype(F32)
        arrived(sum_y_in.at[way, k, d - 1], y_s.at[way, k, d - 1], y_r.at[way, k, d - 1], near(way))
        return sum_y_in[way, k, d - 1]

    def pass_on(d):
        for k in range(NZ):
            for way in range(2):
                if d < reach(way, k):
                    total = incoming(way, k, d + 1) + block(k, step_of[way] * d, 0, CA).astype(F32)
                    sum_y[way, k, d - 1] = total
                    put(sum_y.at[way, k, d - 1], sum_y_in.at[way, k, d - 1], y_s.at[way, k, d - 1], y_r.at[way, k, d - 1], near(way))

    def totals():
        for k in range(NZ - 2, -1, -1):
            arrived(raw_z_in.at[row[k]], zr_s.at[k], zr_r.at[row[k]], at_z(k))
        for d in (4, 3, 5, 2, 6, 1, 7, 0):
            total = block(NZ - 1, d, CA, W - CA).astype(F32)
            for k in range(NZ - 1):
                total += raw_z_in[row[k], d].astype(F32)
            tot_z[d] = total
            if d:
                put(tot_z.at[d], tot_z_in.at[d - 1], zt_s.at[d - 1], zt_r.at[d - 1], at_y(d))

    pass_on(3)
    pass_on(2)
    pass_on(1)
    totals()
    for k in range(NZ):
        total = incoming(0, k, 1) + incoming(1, k, 1) + block(k, 0, 0, CA).astype(F32)
        if k < NZ - 1:
            fin_z[k] = total
            put(fin_z.at[k], fin_z_in.at[z], zf_s.at[k], zf_r.at[z], at_z(k))
        else:
            owned[:, 0:CA] = total
    mine = tot_z[0]
    for d in range(NY - 1):
        arrived(tot_z_in.at[d], zt_s.at[d], zt_r.at[d], at_y(1))
        mine += tot_z_in[d]
    owned[:, CA:W] = mine
    mine = owned[:, 0:CA]
    for k in range(NZ - 1):
        arrived(fin_z_in.at[row[k]], zf_s.at[k], zf_r.at[row[k]], at_z(k))
        mine += fin_z_in[row[k]]
    owned[:, 0:CA] = mine

    root_copy.wait()
    products = jnp.dot(owned[...].astype(BF16), root_v[...], preferred_element_type=F32)
    mine = owned[...]
    grad_norm = jnp.sum(jnp.sum(mine * mine, axis=1, keepdims=True), axis=0, keepdims=True)
    update_norm = jnp.sum(jnp.sum(products * products, axis=1, keepdims=True), axis=0, keepdims=True)
    left = lax.broadcasted_iota(jnp.int32, (1, 128), 1) < 64
    norms[...] = jnp.where(left, grad_norm, update_norm)
    for m in NORM_ORDER:
        put(norms, norms_in.at[m - 1], nb_s.at[m - 1], nb_r.at[m - 1], (lax.bitwise_xor(g, m), r))

    rows_all[g] = mine

    def xat(m):
        return lax.rem(x + m, 4)

    far, sib = gid(x, 1 - zh, c), gid(x, zh, 1 - c)
    put(rows_all.at[g], rows_all.at[g], gz_s, gz_r, (far, r))
    for m in (1, 3, 2):
        put(rows_all.at[g], rows_all.at[g], gx_s.at[0, m], gx_r.at[0, m], (gid(xat(m), zh, c), r))
    put(rows_all.at[g], rows_all.at[g], gc_s.at[0, 0], gc_r.at[0, 0], (sib, r))

    total = norms[...]
    for m in range(15):
        arrived(norms_in.at[m], nb_s.at[m], nb_r.at[m], (sib, r))
        total += norms_in[m]
    graft = jnp.sqrt(total[:, 0:1] / (total[:, 64:65] + 1e-06))
    own_slot = z * NY + y
    gathered[own_slot] = (graft * products).astype(BF16)

    for k in range(NZ - 1):
        put(gathered.at[own_slot], gathered.at[own_slot], cz_s.at[k], cz_r.at[z], at_z(k))

    def slot_from(k, way, hops):
        return gathered.at[row[k] * NY + yy(-step_of[way] * hops)]

    def hop(way, k, h):
        ref = slot_from(k, way, h)
        if h:
            arrived(ref, cy_s.at[way, k, h - 1], cy_r.at[way, k, h - 1], near(way))
        elif way == 0 and k < NZ - 1:
            arrived(gathered.at[row[k] * NY + y], cz_s.at[k], cz_r.at[row[k]], at_z(k))
        if h < reach(way, k):
            put(ref, ref, cy_s.at[way, k, h], cy_r.at[way, k, h], near(way))

    def rows_from(half, m, cc):
        hh = zh if half == 0 else 1 - zh
        return rows_all.at[gid(lax.rem(x + 4 - m, 4), hh, cc)]

    def across(half):
        def go():
            for m in (1, 3, 2):
                ref = rows_from(half, m, c)
                arrived(ref, gx_s.at[half, m], gx_r.at[half, m], (sib, r))
                put(ref, ref, gc_s.at[half, m], gc_r.at[half, m], (sib, r))
        return go

    def far_rows():
        ref = rows_all.at[far]
        arrived(ref, gz_s, gz_r, (far, r))
        for m in (1, 3, 2):
            put(ref, ref, gx_s.at[1, m], gx_r.at[1, m], (gid(xat(m), zh, c), r))
        put(ref, ref, gc_s.at[1, 0], gc_r.at[1, 0], (sib, r))

    def all_rows():
        stat_copy.wait()
        for half in range(2):
            for m in range(4):
                arrived(rows_from(half, m, 1 - c), gc_s.at[half, m], gc_r.at[half, m], (sib, r))
        th[...], tl[...] = split(rows_all[...].reshape(16 * ROWS, W))

    half_rows = W // 2
    halves = [pl.ds(i * half_rows, half_rows) for i in range(2)]

    def rows_dot(a, b):
        return lax.dot_general(a, b, (((0,), (0,)), ((), ())), preferred_element_type=F32)

    def statistic(i):
        def go():
            rows = halves[i]
            gram = rows_dot(th[:, rows], th[...]) + rows_dot(th[:, rows], tl[...]) + rows_dot(tl[:, rows], th[...])
            stat_new = DECAY * stat_v[rows] + (1.0 - DECAY) * gram
            stat_out[0, rows] = stat_new
            count = step[0]
            power = jnp.float32(1.0)
            for n in range(12):
                power = jnp.where(n < count, power * DECAY, power)
            correction = 1.0 / (1.0 - jnp.full((8, 128), power, F32))
            shifted[rows] = stat_new * correction[0:1, 0:1] + jnp.where(eye_block(i * half_rows, half_rows), EPS, 0.0)
        return go

    def frobenius():
        value = shifted[...]
        return jnp.sqrt(jnp.sum(jnp.sum(value * value, axis=1, keepdims=True), axis=0, keepdims=True))

    def factor_from(i, coupled):
        rows = halves[i]
        mh[rows], ml[rows] = split(coupled)
        th[rows], tl[rows] = split((jnp.where(eye_block(i * half_rows, half_rows), 5.0, 0.0) - coupled) * 0.25)

    norm_of = []

    def start_newton():
        norm_of.append(frobenius())
        for i in range(2):
            factor_from(i, shifted[halves[i]] / norm_of[0])
            xh[halves[i]], xl[halves[i]] = th[halves[i]], tl[halves[i]]

    def product(a_high, a_low, b_high, b_low, give):
        def piece(i):
            def go():
                rows = halves[i]
                out = jnp.dot(a_high[rows], b_high[...], preferred_element_type=F32)
                out += jnp.dot(a_high[rows], b_low[...], preferred_element_type=F32)
                out += jnp.dot(a_low[rows], b_high[...], preferred_element_type=F32)
                give(i, rows, out)
            return go
        return [piece(0), piece(1)]

    def keep(high_ref, low_ref):
        def give(i, rows, out):
            high_ref[rows], low_ref[rows] = split(out)
        return give

    def couple(i, rows, out):
        shifted[rows] = out

    def next_factor():
        for i in range(2):
            factor_from(i, shifted[halves[i]])

    def take_x():
        xh[...], xl[...] = qh[...], ql[...]

    def finish(i, rows, out):
        root_out[0, rows] = (out / jnp.sqrt(jnp.sqrt(norm_of[0]))).astype(BF16)

    work = [all_rows, statistic(0), statistic(1), start_newton]
    for repeat in range(ITERS):
        last = repeat + 1 == ITERS
        if repeat:
            work += product(xh, xl, th, tl, finish if last else keep(qh, ql))
            if not last:
                work.append(take_x)
        if not last:
            work += product(th, tl, th, tl, keep(qh, ql))
            work += product(qh, ql, qh, ql, keep(th, tl))
            work += product(th, tl, mh, ml, couple)
            work.append(next_factor)

    ends = [(way, k, reach(way, k)) for k in (3, 2, 4, 5, 1, 0) for way in range(2)]
    for place, (way, k, h) in enumerate(RING + tuple(ends)):
        if place == AT_ACROSS:
            across(0)()
        if place == AT_FAR:
            far_rows()
        if place == AT_ACROSS_FAR:
            across(1)()
        if place >= AT_WORK and work:
            work.pop(0)()
        hop(way, k, h)
    for piece in work:
        piece()

    for copy in started:
        copy.wait_send()


def place_kernel(order, slots, stat, root, update, stat_out, root_out, sems):
    def update_copy(j):
        return pltpu.make_async_copy(slots.at[j], update.at[order[j]], sems.at[j])

    others = [
        pltpu.make_async_copy(stat, stat_out, sems.at[NB]),
        pltpu.make_async_copy(root, root_out, sems.at[NB + 1]),
    ]
    for copy in others:
        copy.start()
    for j in range(NB):
        update_copy(j).start()
    for copy in others:
        copy.wait()
    for j in range(NB):
        update_copy(j).wait()


def local(grad_parts, owner_order, step_count, stat_old, root_old):
    smem = pl.BlockSpec(memory_space=pltpu.SMEM)
    vmem = pl.BlockSpec(memory_space=pltpu.VMEM)
    hbm = pl.BlockSpec(memory_space=pltpu.HBM)
    sem = pltpu.SemaphoreType.DMA
    square = pltpu.VMEM((W, W), BF16)
    shapes = (
        jax.ShapeDtypeStruct((NB, ROWS, W), BF16),
        jax.ShapeDtypeStruct((1, W, W), F32),
        jax.ShapeDtypeStruct((1, W, W), BF16),
    )
    slots, stat_new, root_new = pl.pallas_call(
        kernel,
        out_shape=shapes,
        in_specs=[smem, hbm, hbm, hbm, hbm],
        out_specs=(vmem, vmem, vmem),
        scratch_shapes=[
            pltpu.SMEM((NB,), jnp.int32),
            pltpu.VMEM((NB, ROWS, W), BF16),
            pltpu.VMEM((2, NZ, ROWS, CA), BF16),
            pltpu.VMEM((2, NZ, ROWS, CA), BF16),
            pltpu.VMEM((2, NZ, 3, ROWS, CA), F32),
            pltpu.VMEM((2, NZ, 3, ROWS, CA), F32),
            pltpu.VMEM((NZ - 1, NY, ROWS, W - CA), BF16),
            pltpu.VMEM((NZ, NY, ROWS, W - CA), BF16),
            pltpu.VMEM((NY, ROWS, W - CA), F32),
            pltpu.VMEM((NY - 1, ROWS, W - CA), F32),
            pltpu.VMEM((NZ - 1, ROWS, CA), F32),
            pltpu.VMEM((NZ, ROWS, CA), F32),
            pltpu.VMEM((ROWS, W), F32),
            pltpu.VMEM((1, 128), F32),
            pltpu.VMEM((15, 1, 128), F32),
            pltpu.VMEM((16, ROWS, W), F32),
            pltpu.VMEM((W, W), F32),
            pltpu.VMEM((W, W), BF16),
            square, square, square, square, square, square, square, square,
            pltpu.VMEM((W, W), F32),
            sem((2, NZ, 4)), sem((2, NZ, 4)),
            sem((NZ - 1,)), sem((NZ,)),
            sem((NY - 1,)), sem((NY - 1,)),
            sem((NZ - 1,)), sem((NZ,)),
            sem((15,)), sem((15,)),
            sem((2, 4)), sem((2, 4)),
            sem((2, 4)), sem((2, 4)),
            sem, sem,
            sem((NZ - 1,)), sem((NZ,)),
            sem((2, NZ, 4)), sem((2, NZ, 4)),
            sem((4,)),
        ],
        compiler_params=pltpu.CompilerParams(
            collective_id=0, has_side_effects=True, vmem_limit_bytes=48 * 2**20
        ),
        name="shampoo_step",
    )(step_count, *(pltpu.with_memory_space_constraint(a, pltpu.HBM) for a in (owner_order, grad_parts, stat_old, root_old)))
    return pl.pallas_call(
        place_kernel,
        out_shape=shapes,
        in_specs=[smem, vmem, vmem, vmem],
        out_specs=(hbm, hbm, hbm),
        scratch_shapes=[sem((NB + 2,))],
        compiler_params=pltpu.CompilerParams(vmem_limit_bytes=8 * 2**20),
        name="place",
    )(owner_order, slots, stat_new, root_new)


def solution(mesh):
    placed = (
        P("replica", None, "group", None),
        P(),
        P(),
        P("replica", None, None),
        P("replica", None, None),
    )
    return jax.shard_map(
        local,
        mesh=mesh,
        in_specs=placed,
        out_specs=(P(None, "group", None), P("replica", None, None), P("replica", None, None)),
        check_vma=False,
    )
```

```python
import jax
import jax.numpy as jnp
from jax import lax
from jax.experimental import pallas as pl
from jax.experimental.pallas import tpu as pltpu
from jax.sharding import PartitionSpec as P

DECAY = 0.95
EPS = 0.001
NY, NZ = 8, 6
NB, ROWS, W = 48, 32, 512
NORM_ORDER = (10, 11, 14, 15, 2, 3, 6, 7, 8, 9, 12, 13, 4, 5, 1)
AT_ACROSS, AT_NEAR, AT_FAR, AT_ACROSS_FAR, AT_WORK = 2, 6, 10, 22, 26
CA = 384
F32, BF16 = jnp.float32, jnp.bfloat16


def split(value):
    high = value.astype(BF16)
    return high, (value - high.astype(F32)).astype(BF16)


def eye_block(first, rows):
    row = lax.broadcasted_iota(jnp.int32, (rows, W), 0) + first
    return row == lax.broadcasted_iota(jnp.int32, (rows, W), 1)


FAR = ((5, 4, 3, 2, 1, 0), (5, 4, 3, 0, 2, 1), (5, 0, 4, 1, 3, 2), (0, 5, 1, 4, 2, 3), (0, 1, 2, 5, 3, 4), (0, 1, 2, 3, 4, 5))
RING = (
    (0, 5, 0), (1, 5, 0), (0, 4, 0), (1, 4, 0), (0, 3, 0), (1, 3, 0), (0, 2, 0), (1, 2, 0), (0, 5, 1), (1, 5, 1),
    (0, 1, 0), (1, 1, 0), (0, 0, 0), (1, 0, 0), (0, 4, 1), (1, 3, 1), (0, 2, 1), (1, 2, 1), (0, 3, 1), (1, 4, 1),
    (0, 1, 1), (1, 1, 1), (0, 0, 1), (1, 0, 1), (0, 4, 2), (1, 3, 2), (1, 5, 2), (0, 2, 2), (1, 2, 2), (0, 3, 2),
    (0, 1, 2), (1, 1, 2), (0, 0, 2), (1, 0, 2), (0, 4, 3), (1, 3, 3), (0, 2, 3), (1, 4, 2), (0, 5, 2), (1, 5, 3),
    (1, 1, 3), (0, 0, 3),
)


def kernel(
    step, order_hbm, gp_hbm, stat_hbm, root_hbm,
    gathered, stat_out, root_out,
    order, gp,
    raw_y, raw_y_in, sum_y, sum_y_in, raw_z, raw_z_in, tot_z, tot_z_in, fin_z, fin_z_in,
    owned, norms, norms_in, rows_all, stat_v, root_v,
    th, tl, mh, ml, qh, ql, xh, xl, shifted,
    y_s, y_r, zr_s, zr_r, zt_s, zt_r, zf_s, zf_r, nb_s, nb_r, gx_s, gx_r, gc_s, gc_r, gz_s, gz_r,
    cz_s, cz_r, cy_s, cy_r, loc,
):
    gp_copy = pltpu.make_async_copy(gp_hbm.at[0], gp, loc.at[2])
    order_copy = pltpu.make_async_copy(order_hbm, order, loc.at[3])
    order_copy.start()
    gp_copy.start()
    g, r = lax.axis_index("group"), lax.axis_index("replica")
    x, zh, c = g // 4, lax.rem(g // 2, 2), lax.rem(g, 2)
    z, y = r // NY, lax.rem(r, NY)
    is_z = [(NZ - lax.rem(z + NZ - v, NZ)) // NZ for v in range(NZ)]
    row = [sum(FAR[v][k] * is_z[v] for v in range(NZ)) for k in range(NZ - 1)] + [z]

    def gid(xx, hh, cc):
        return xx * 4 + hh * 2 + cc

    def yy(d):
        return lax.rem(y + d + NY, NY)

    def at_y(d):
        return g, z * NY + yy(d)

    def at_z(k):
        return g, row[k] * NY + y

    started = []

    def describe(src, dst, ss, rs, dev):
        return pltpu.make_async_remote_copy(
            src_ref=src, dst_ref=dst, send_sem=ss, recv_sem=rs,
            device_id=dev, device_id_type=pl.DeviceIdType.MESH,
        )

    def put(src, dst, ss, rs, dev):
        copy = describe(src, dst, ss, rs, dev)
        copy.start()
        started.append(copy)

    def arrived(dst, ss, rs, dev):
        describe(dst, dst, ss, rs, dev).wait_recv()

    stat_copy = pltpu.make_async_copy(stat_hbm.at[0], stat_v, loc.at[0])
    root_copy = pltpu.make_async_copy(root_hbm.at[0], root_v, loc.at[1])
    barrier = pltpu.get_barrier_semaphore()
    peers = [at_y(d) for d in range(1, NY)] + [at_z(k) for k in range(NZ - 1)]
    peers += [(lax.bitwise_xor(g, m), r) for m in range(1, 16)]
    for dev in peers:
        pl.semaphore_signal(barrier, inc=1, device_id=dev, device_id_type=pl.DeviceIdType.MESH)
    stat_copy.start()
    root_copy.start()
    order_copy.wait()
    gp_copy.wait()

    def block(k, d, first, width):
        return gp[order[row[k] * NY + yy(d)], :, pl.ds(first, width)]

    def reach(way, k):
        return 4 if (way + k) % 2 == 0 else 3

    step_of = (1, -1)
    for k in range(NZ):
        for way in range(2):
            raw_y[way, k] = block(k, step_of[way] * reach(way, k), 0, CA)
    for k in range(NZ - 1):
        for d in range(NY):
            raw_z[k, d] = block(k, d, CA, W - CA)
    pl.semaphore_wait(barrier, len(peers))

    def near(way):
        return at_y(step_of[way])

    for k in range(NZ):
        for way in range(2):
            at = reach(way, k) - 1
            put(raw_y.at[way, k], raw_y_in.at[way, k], y_s.at[way, k, at], y_r.at[way, k, at], near(way))
    for k in range(NZ - 1):
        put(raw_z.at[k], raw_z_in.at[z], zr_s.at[k], zr_r.at[z], at_z(k))

    def incoming(way, k, d):
        if d == reach(way, k):
            arrived(raw_y_in.at[way, k], y_s.at[way, k, d - 1], y_r.at[way, k, d - 1], near(way))
            return raw_y_in[way, k].astype(F32)
        arrived(sum_y_in.at[way, k, d - 1], y_s.at[way, k, d - 1], y_r.at[way, k, d - 1], near(way))
        return sum_y_in[way, k, d - 1]

    def pass_on(d):
        for k in range(NZ):
            for way in range(2):
                if d < reach(way, k):
                    total = incoming(way, k, d + 1) + block(k, step_of[way] * d, 0, CA).astype(F32)
                    sum_y[way, k, d - 1] = total
                    put(sum_y.at[way, k, d - 1], sum_y_in.at[way, k, d - 1], y_s.at[way, k, d - 1], y_r.at[way, k, d - 1], near(way))

    def totals():
        for k in range(NZ - 2, -1, -1):
            arrived(raw_z_in.at[row[k]], zr_s.at[k], zr_r.at[row[k]], at_z(k))
        for d in (4, 3, 5, 2, 6, 1, 7, 0):
            total = block(NZ - 1, d, CA, W - CA).astype(F32)
            for k in range(NZ - 1):
                total += raw_z_in[row[k], d].astype(F32)
            tot_z[d] = total
            if d:
                put(tot_z.at[d], tot_z_in.at[d - 1], zt_s.at[d - 1], zt_r.at[d - 1], at_y(d))

    pass_on(3)
    pass_on(2)
    pass_on(1)
    totals()
    for k in range(NZ):
        total = incoming(0, k, 1) + incoming(1, k, 1) + block(k, 0, 0, CA).astype(F32)
        if k < NZ - 1:
            fin_z[k] = total
            put(fin_z.at[k], fin_z_in.at[z], zf_s.at[k], zf_r.at[z], at_z(k))
        else:
            owned[:, 0:CA] = total
    mine = tot_z[0]
    for d in range(NY - 1):
        arrived(tot_z_in.at[d], zt_s.at[d], zt_r.at[d], at_y(1))
        mine += tot_z_in[d]
    owned[:, CA:W] = mine
    mine = owned[:, 0:CA]
    for k in range(NZ - 1):
        arrived(fin_z_in.at[row[k]], zf_s.at[k], zf_r.at[row[k]], at_z(k))
        mine += fin_z_in[row[k]]
    owned[:, 0:CA] = mine

    root_copy.wait()
    products = jnp.dot(owned[...].astype(BF16), root_v[...], preferred_element_type=F32)
    mine = owned[...]
    grad_norm = jnp.sum(jnp.sum(mine * mine, axis=1, keepdims=True), axis=0, keepdims=True)
    update_norm = jnp.sum(jnp.sum(products * products, axis=1, keepdims=True), axis=0, keepdims=True)
    left = lax.broadcasted_iota(jnp.int32, (1, 128), 1) < 64
    norms[...] = jnp.where(left, grad_norm, update_norm)
    for m in NORM_ORDER:
        put(norms, norms_in.at[m - 1], nb_s.at[m - 1], nb_r.at[m - 1], (lax.bitwise_xor(g, m), r))

    rows_all[g] = mine

    def xat(m):
        return lax.rem(x + m, 4)

    far, sib = gid(x, 1 - zh, c), gid(x, zh, 1 - c)
    put(rows_all.at[g], rows_all.at[g], gz_s, gz_r, (far, r))
    for m in (1, 3, 2):
        put(rows_all.at[g], rows_all.at[g], gx_s.at[0, m], gx_r.at[0, m], (gid(xat(m), zh, c), r))
    put(rows_all.at[g], rows_all.at[g], gc_s.at[0, 0], gc_r.at[0, 0], (sib, r))

    total = norms[...]
    for m in range(15):
        arrived(norms_in.at[m], nb_s.at[m], nb_r.at[m], (sib, r))
        total += norms_in[m]
    graft = jnp.sqrt(total[:, 0:1] / (total[:, 64:65] + 1e-06))
    own_slot = z * NY + y
    gathered[own_slot] = (graft * products).astype(BF16)

    for k in range(NZ - 1):
        put(gathered.at[own_slot], gathered.at[own_slot], cz_s.at[k], cz_r.at[z], at_z(k))

    def slot_from(k, way, hops):
        return gathered.at[row[k] * NY + yy(-step_of[way] * hops)]

    def hop(way, k, h):
        ref = slot_from(k, way, h)
        if h:
            arrived(ref, cy_s.at[way, k, h - 1], cy_r.at[way, k, h - 1], near(way))
        elif way == 0 and k < NZ - 1:
            arrived(gathered.at[row[k] * NY + y], cz_s.at[k], cz_r.at[row[k]], at_z(k))
        if h < reach(way, k):
            put(ref, ref, cy_s.at[way, k, h], cy_r.at[way, k, h], near(way))

    def rows_from(half, m, cc):
        hh = zh if half == 0 else 1 - zh
        return rows_all.at[gid(lax.rem(x + 4 - m, 4), hh, cc)]

    def across(half):
        def go():
            for m in (1, 3, 2):
                ref = rows_from(half, m, c)
                arrived(ref, gx_s.at[half, m], gx_r.at[half, m], (sib, r))
                put(ref, ref, gc_s.at[half, m], gc_r.at[half, m], (sib, r))
        return go

    def far_rows():
        ref = rows_all.at[far]
        arrived(ref, gz_s, gz_r, (far, r))
        for m in (1, 3, 2):
            put(ref, ref, gx_s.at[1, m], gx_r.at[1, m], (gid(xat(m), zh, c), r))
        put(ref, ref, gc_s.at[1, 0], gc_r.at[1, 0], (sib, r))

    def take_rows(half):
        def go():
            for m in range(4):
                arrived(rows_from(half, m, 1 - c), gc_s.at[half, m], gc_r.at[half, m], (sib, r))
            for xx in range(4):
                rows = pl.ds((4 * half + xx) * 2 * ROWS, 2 * ROWS)
                pair = rows_all[pl.ds(gid(xx, zh if half == 0 else 1 - zh, 0), 2)]
                th[rows], tl[rows] = split(pair.reshape(2 * ROWS, W))
        return go

    half_rows = W // 2
    halves = [pl.ds(i * half_rows, half_rows) for i in range(2)]

    def rows_dot(a, b):
        return lax.dot_general(a, b, (((0,), (0,)), ((), ())), preferred_element_type=F32)

    def gram_of(half, i):
        some, rows = halves[half], halves[i]
        gram = rows_dot(th[some, rows], th[some]) + rows_dot(th[some, rows], tl[some])
        return gram + rows_dot(tl[some, rows], th[some])

    def near_gram(i):
        def go():
            shifted[halves[i]] = gram_of(0, i)
        return go

    def statistic(i):
        def go():
            rows = halves[i]
            gram = shifted[rows] + gram_of(1, i)
            if i == 0:
                stat_copy.wait()
            stat_new = DECAY * stat_v[rows] + (1.0 - DECAY) * gram
            stat_out[0, rows] = stat_new
            count = step[0]
            power = jnp.float32(1.0)
            for n in range(12):
                power = jnp.where(n < count, power * DECAY, power)
            correction = 1.0 / (1.0 - jnp.full((8, 128), power, F32))
            shifted[rows] = stat_new * correction[0:1, 0:1] + jnp.where(eye_block(i * half_rows, half_rows), EPS, 0.0)
        return go

    def frobenius():
        value = shifted[...]
        return jnp.sqrt(jnp.sum(jnp.sum(value * value, axis=1, keepdims=True), axis=0, keepdims=True))

    def factor_from(i, coupled, high, low, keep_coupled=True):
        rows = halves[i]
        if keep_coupled:
            mh[rows], ml[rows] = split(coupled)
        high[rows], low[rows] = split((jnp.where(eye_block(i * half_rows, half_rows), 5.0, 0.0) - coupled) * 0.25)

    norm_of = []

    def start_newton():
        norm_of.append(frobenius())
        for i in range(2):
            factor_from(i, shifted[halves[i]] / norm_of[0], xh, xl)

    def product(a_high, a_low, b_high, b_low, give):
        def piece(i):
            def go():
                rows = halves[i]
                out = jnp.dot(a_high[rows], b_high[...], preferred_element_type=F32)
                out += jnp.dot(a_high[rows], b_low[...], preferred_element_type=F32)
                out += jnp.dot(a_low[rows], b_high[...], preferred_element_type=F32)
                give(i, rows, out)
            return go
        return [piece(0), piece(1)]

    def keep(high_ref, low_ref):
        def give(i, rows, out):
            high_ref[rows], low_ref[rows] = split(out)
        return give

    def couple(i, rows, out):
        shifted[rows] = out

    def next_factor(keep_coupled):
        def go():
            for i in range(2):
                factor_from(i, shifted[halves[i]], th, tl, keep_coupled)
        return go

    def finish(i, rows, out):
        root_out[0, rows] = (out / jnp.sqrt(jnp.sqrt(norm_of[0]))).astype(BF16)

    work = [take_rows(1), statistic(0), statistic(1), start_newton]
    work += product(xh, xl, xh, xl, keep(qh, ql)) + product(qh, ql, qh, ql, keep(th, tl))
    work += product(th, tl, mh, ml, couple) + [next_factor(True)]
    work += product(xh, xl, th, tl, keep(qh, ql)) + product(th, tl, th, tl, keep(xh, xl))
    work += product(xh, xl, xh, xl, keep(th, tl)) + product(th, tl, mh, ml, couple) + [next_factor(False)]
    work += product(qh, ql, th, tl, finish)

    ends = [(way, k, reach(way, k)) for k in (3, 2, 4, 5, 1, 0) for way in range(2)]
    for place, (way, k, h) in enumerate(RING + tuple(ends)):
        if place == AT_ACROSS:
            across(0)()
        if place == AT_NEAR:
            take_rows(0)()
        if place in (AT_NEAR + 1, AT_NEAR + 2):
            near_gram(place - AT_NEAR - 1)()
        if place == AT_FAR:
            far_rows()
        if place == AT_ACROSS_FAR:
            across(1)()
        if place >= AT_WORK and work:
            work.pop(0)()
        hop(way, k, h)
    for piece in work:
        piece()

    for copy in started:
        copy.wait_send()


def place_kernel(order, slots, stat, root, update, stat_out, root_out, sems):
    def update_copy(j):
        return pltpu.make_async_copy(slots.at[j], update.at[order[j]], sems.at[j])

    others = [
        pltpu.make_async_copy(stat, stat_out, sems.at[NB]),
        pltpu.make_async_copy(root, root_out, sems.at[NB + 1]),
    ]
    for copy in others:
        copy.start()
    for j in range(NB):
        update_copy(j).start()
    for copy in others:
        copy.wait()
    for j in range(NB):
        update_copy(j).wait()


def local(grad_parts, owner_order, step_count, stat_old, root_old):
    smem = pl.BlockSpec(memory_space=pltpu.SMEM)
    vmem = pl.BlockSpec(memory_space=pltpu.VMEM)
    hbm = pl.BlockSpec(memory_space=pltpu.HBM)
    sem = pltpu.SemaphoreType.DMA
    square = pltpu.VMEM((W, W), BF16)
    shapes = (
        jax.ShapeDtypeStruct((NB, ROWS, W), BF16),
        jax.ShapeDtypeStruct((1, W, W), F32),
        jax.ShapeDtypeStruct((1, W, W), BF16),
    )
    slots, stat_new, root_new = pl.pallas_call(
        kernel,
        out_shape=shapes,
        in_specs=[smem, hbm, hbm, hbm, hbm],
        out_specs=(vmem, vmem, vmem),
        scratch_shapes=[
            pltpu.SMEM((NB,), jnp.int32),
            pltpu.VMEM((NB, ROWS, W), BF16),
            pltpu.VMEM((2, NZ, ROWS, CA), BF16),
            pltpu.VMEM((2, NZ, ROWS, CA), BF16),
            pltpu.VMEM((2, NZ, 3, ROWS, CA), F32),
            pltpu.VMEM((2, NZ, 3, ROWS, CA), F32),
            pltpu.VMEM((NZ - 1, NY, ROWS, W - CA), BF16),
            pltpu.VMEM((NZ, NY, ROWS, W - CA), BF16),
            pltpu.VMEM((NY, ROWS, W - CA), F32),
            pltpu.VMEM((NY - 1, ROWS, W - CA), F32),
            pltpu.VMEM((NZ - 1, ROWS, CA), F32),
            pltpu.VMEM((NZ, ROWS, CA), F32),
            pltpu.VMEM((ROWS, W), F32),
            pltpu.VMEM((1, 128), F32),
            pltpu.VMEM((15, 1, 128), F32),
            pltpu.VMEM((16, ROWS, W), F32),
            pltpu.VMEM((W, W), F32),
            pltpu.VMEM((W, W), BF16),
            square, square, square, square, square, square, square, square,
            pltpu.VMEM((W, W), F32),
            sem((2, NZ, 4)), sem((2, NZ, 4)),
            sem((NZ - 1,)), sem((NZ,)),
            sem((NY - 1,)), sem((NY - 1,)),
            sem((NZ - 1,)), sem((NZ,)),
            sem((15,)), sem((15,)),
            sem((2, 4)), sem((2, 4)),
            sem((2, 4)), sem((2, 4)),
            sem, sem,
            sem((NZ - 1,)), sem((NZ,)),
            sem((2, NZ, 4)), sem((2, NZ, 4)),
            sem((4,)),
        ],
        compiler_params=pltpu.CompilerParams(
            collective_id=0, has_side_effects=True, vmem_limit_bytes=48 * 2**20
        ),
        name="shampoo_step",
    )(step_count, *(pltpu.with_memory_space_constraint(a, pltpu.HBM) for a in (owner_order, grad_parts, stat_old, root_old)))
    return pl.pallas_call(
        place_kernel,
        out_shape=shapes,
        in_specs=[smem, vmem, vmem, vmem],
        out_specs=(hbm, hbm, hbm),
        scratch_shapes=[sem((NB + 2,))],
        compiler_params=pltpu.CompilerParams(vmem_limit_bytes=8 * 2**20),
        name="place",
    )(owner_order, slots, stat_new, root_new)


def solution(mesh):
    placed = (
        P("replica", None, "group", None),
        P(),
        P(),
        P("replica", None, None),
        P("replica", None, None),
    )
    return jax.shard_map(
        local,
        mesh=mesh,
        in_specs=placed,
        out_specs=(P(None, "group", None), P("replica", None, None), P("replica", None, None)),
        check_vma=False,
    )
```

```python
import jax
import jax.numpy as jnp
from jax import lax
from jax.experimental import pallas as pl
from jax.experimental.pallas import tpu as pltpu
from jax.sharding import PartitionSpec as P

DECAY = 0.95
EPS = 0.001
NY, NZ = 8, 6
NB, ROWS, W = 48, 32, 512
NORM_ORDER = (10, 11, 14, 15, 2, 3, 6, 7, 8, 9, 12, 13, 4, 5, 1)
AT_ACROSS, AT_NEAR, AT_FAR, AT_ACROSS_FAR, AT_WORK = 2, 6, 10, 22, 26
CA = 384
F32, BF16 = jnp.float32, jnp.bfloat16


def split(value):
    high = value.astype(BF16)
    return high, (value - high.astype(F32)).astype(BF16)


def eye_block(first, rows):
    row = lax.broadcasted_iota(jnp.int32, (rows, W), 0) + first
    return row == lax.broadcasted_iota(jnp.int32, (rows, W), 1)


FAR = ((5, 4, 3, 2, 1, 0), (5, 4, 3, 0, 2, 1), (5, 0, 4, 1, 3, 2), (0, 5, 1, 4, 2, 3), (0, 1, 2, 5, 3, 4), (0, 1, 2, 3, 4, 5))
RING = (
    (0, 5, 0), (1, 5, 0), (0, 4, 0), (1, 4, 0), (0, 3, 0), (1, 3, 0), (0, 2, 0), (1, 2, 0), (0, 5, 1), (1, 5, 1),
    (0, 1, 0), (1, 1, 0), (0, 0, 0), (1, 0, 0), (0, 4, 1), (1, 3, 1), (0, 2, 1), (1, 2, 1), (0, 3, 1), (1, 4, 1),
    (0, 1, 1), (1, 1, 1), (0, 0, 1), (1, 0, 1), (0, 4, 2), (1, 3, 2), (1, 5, 2), (0, 2, 2), (1, 2, 2), (0, 3, 2),
    (0, 1, 2), (1, 1, 2), (0, 0, 2), (1, 0, 2), (0, 4, 3), (1, 3, 3), (0, 2, 3), (1, 4, 2), (0, 5, 2), (1, 5, 3),
    (1, 1, 3), (0, 0, 3),
)


def kernel(
    step, order_hbm, gp_hbm, stat_hbm, root_hbm,
    gathered, stat_out, root_out,
    order, gp,
    raw_y, raw_y_in, sum_y, sum_y_in, raw_z, raw_z_in, tot_z, tot_z_in, fin_z, fin_z_in,
    owned, norms, norms_in, rows_all, stat_v, root_v,
    th, tl, mh, ml, qh, ql, xh, xl, shifted,
    y_s, y_r, zr_s, zr_r, zt_s, zt_r, zf_s, zf_r, nb_s, nb_r, gx_s, gx_r, gc_s, gc_r, gz_s, gz_r,
    cz_s, cz_r, cy_s, cy_r, loc,
):
    gp_copy = pltpu.make_async_copy(gp_hbm.at[0], gp, loc.at[2])
    order_copy = pltpu.make_async_copy(order_hbm, order, loc.at[3])
    order_copy.start()
    gp_copy.start()
    g, r = lax.axis_index("group"), lax.axis_index("replica")
    x, zh, c = g // 4, lax.rem(g // 2, 2), lax.rem(g, 2)
    z, y = r // NY, lax.rem(r, NY)
    is_z = [(NZ - lax.rem(z + NZ - v, NZ)) // NZ for v in range(NZ)]
    row = [sum(FAR[v][k] * is_z[v] for v in range(NZ)) for k in range(NZ - 1)] + [z]

    def gid(xx, hh, cc):
        return xx * 4 + hh * 2 + cc

    def yy(d):
        return lax.rem(y + d + NY, NY)

    def at_y(d):
        return g, z * NY + yy(d)

    def at_z(k):
        return g, row[k] * NY + y

    started = []

    def describe(src, dst, ss, rs, dev):
        return pltpu.make_async_remote_copy(
            src_ref=src, dst_ref=dst, send_sem=ss, recv_sem=rs,
            device_id=dev, device_id_type=pl.DeviceIdType.MESH,
        )

    def put(src, dst, ss, rs, dev):
        copy = describe(src, dst, ss, rs, dev)
        copy.start()
        started.append(copy)

    def arrived(dst, ss, rs, dev):
        describe(dst, dst, ss, rs, dev).wait_recv()

    stat_copy = pltpu.make_async_copy(stat_hbm.at[0], stat_v, loc.at[0])
    root_copy = pltpu.make_async_copy(root_hbm.at[0], root_v, loc.at[1])
    barrier = pltpu.get_barrier_semaphore()
    peers = [at_y(d) for d in range(1, NY)] + [at_z(k) for k in range(NZ - 1)]
    peers += [(lax.bitwise_xor(g, m), r) for m in range(1, 16)]
    for dev in peers:
        pl.semaphore_signal(barrier, inc=1, device_id=dev, device_id_type=pl.DeviceIdType.MESH)
    stat_copy.start()
    root_copy.start()
    order_copy.wait()
    gp_copy.wait()

    def block(k, d, first, width):
        return gp[order[row[k] * NY + yy(d)], :, pl.ds(first, width)]

    def reach(way, k):
        return 4 if (way + k) % 2 == 0 else 3

    step_of = (1, -1)
    for k in range(NZ):
        for way in range(2):
            raw_y[way, k] = block(k, step_of[way] * reach(way, k), 0, CA)
    for k in range(NZ - 1):
        for d in range(NY):
            raw_z[k, d] = block(k, d, CA, W - CA)
    pl.semaphore_wait(barrier, len(peers))

    def near(way):
        return at_y(step_of[way])

    for k in range(NZ):
        for way in range(2):
            at = reach(way, k) - 1
            put(raw_y.at[way, k], raw_y_in.at[way, k], y_s.at[way, k, at], y_r.at[way, k, at], near(way))
    for k in range(NZ - 1):
        put(raw_z.at[k], raw_z_in.at[z], zr_s.at[k], zr_r.at[z], at_z(k))

    def incoming(way, k, d):
        if d == reach(way, k):
            arrived(raw_y_in.at[way, k], y_s.at[way, k, d - 1], y_r.at[way, k, d - 1], near(way))
            return raw_y_in[way, k].astype(F32)
        arrived(sum_y_in.at[way, k, d - 1], y_s.at[way, k, d - 1], y_r.at[way, k, d - 1], near(way))
        return sum_y_in[way, k, d - 1]

    def pass_on(d):
        for k in range(NZ):
            for way in range(2):
                if d < reach(way, k):
                    total = incoming(way, k, d + 1) + block(k, step_of[way] * d, 0, CA).astype(F32)
                    sum_y[way, k, d - 1] = total
                    put(sum_y.at[way, k, d - 1], sum_y_in.at[way, k, d - 1], y_s.at[way, k, d - 1], y_r.at[way, k, d - 1], near(way))

    def totals():
        for k in range(NZ - 2, -1, -1):
            arrived(raw_z_in.at[row[k]], zr_s.at[k], zr_r.at[row[k]], at_z(k))
        for d in (4, 3, 5, 2, 6, 1, 7, 0):
            total = block(NZ - 1, d, CA, W - CA).astype(F32)
            for k in range(NZ - 1):
                total += raw_z_in[row[k], d].astype(F32)
            tot_z[d] = total
            if d:
                put(tot_z.at[d], tot_z_in.at[d - 1], zt_s.at[d - 1], zt_r.at[d - 1], at_y(d))

    pass_on(3)
    pass_on(2)
    pass_on(1)
    for k in range(NZ):
        if k == NZ // 2:
            totals()
        total = incoming(0, k, 1) + incoming(1, k, 1) + block(k, 0, 0, CA).astype(F32)
        if k < NZ - 1:
            fin_z[k] = total
            put(fin_z.at[k], fin_z_in.at[z], zf_s.at[k], zf_r.at[z], at_z(k))
        else:
            owned[:, 0:CA] = total
    mine = tot_z[0]
    for d in range(NY - 1):
        arrived(tot_z_in.at[d], zt_s.at[d], zt_r.at[d], at_y(1))
        mine += tot_z_in[d]
    owned[:, CA:W] = mine
    mine = owned[:, 0:CA]
    for k in range(NZ - 1):
        arrived(fin_z_in.at[row[k]], zf_s.at[k], zf_r.at[row[k]], at_z(k))
        mine += fin_z_in[row[k]]
    owned[:, 0:CA] = mine

    root_copy.wait()
    products = jnp.dot(owned[...].astype(BF16), root_v[...], preferred_element_type=F32)
    mine = owned[...]
    grad_norm = jnp.sum(jnp.sum(mine * mine, axis=1, keepdims=True), axis=0, keepdims=True)
    update_norm = jnp.sum(jnp.sum(products * products, axis=1, keepdims=True), axis=0, keepdims=True)
    left = lax.broadcasted_iota(jnp.int32, (1, 128), 1) < 64
    norms[...] = jnp.where(left, grad_norm, update_norm)
    for m in NORM_ORDER:
        put(norms, norms_in.at[m - 1], nb_s.at[m - 1], nb_r.at[m - 1], (lax.bitwise_xor(g, m), r))

    rows_all[g] = mine

    def xat(m):
        return lax.rem(x + m, 4)

    far, sib = gid(x, 1 - zh, c), gid(x, zh, 1 - c)
    put(rows_all.at[g], rows_all.at[g], gz_s, gz_r, (far, r))
    for m in (1, 3, 2):
        put(rows_all.at[g], rows_all.at[g], gx_s.at[0, m], gx_r.at[0, m], (gid(xat(m), zh, c), r))
    put(rows_all.at[g], rows_all.at[g], gc_s.at[0, 0], gc_r.at[0, 0], (sib, r))

    total = norms[...]
    for m in range(15):
        arrived(norms_in.at[m], nb_s.at[m], nb_r.at[m], (sib, r))
        total += norms_in[m]
    graft = jnp.sqrt(total[:, 0:1] / (total[:, 64:65] + 1e-06))
    own_slot = z * NY + y
    gathered[own_slot] = (graft * products).astype(BF16)

    for k in range(NZ - 1):
        put(gathered.at[own_slot], gathered.at[own_slot], cz_s.at[k], cz_r.at[z], at_z(k))

    def slot_from(k, way, hops):
        return gathered.at[row[k] * NY + yy(-step_of[way] * hops)]

    def hop(way, k, h):
        ref = slot_from(k, way, h)
        if h:
            arrived(ref, cy_s.at[way, k, h - 1], cy_r.at[way, k, h - 1], near(way))
        elif way == 0 and k < NZ - 1:
            arrived(gathered.at[row[k] * NY + y], cz_s.at[k], cz_r.at[row[k]], at_z(k))
        if h < reach(way, k):
            put(ref, ref, cy_s.at[way, k, h], cy_r.at[way, k, h], near(way))

    def rows_from(half, m, cc):
        hh = zh if half == 0 else 1 - zh
        return rows_all.at[gid(lax.rem(x + 4 - m, 4), hh, cc)]

    def across(half):
        def go():
            for m in (1, 3, 2):
                ref = rows_from(half, m, c)
                arrived(ref, gx_s.at[half, m], gx_r.at[half, m], (sib, r))
                put(ref, ref, gc_s.at[half, m], gc_r.at[half, m], (sib, r))
        return go

    def far_rows():
        ref = rows_all.at[far]
        arrived(ref, gz_s, gz_r, (far, r))
        for m in (1, 3, 2):
            put(ref, ref, gx_s.at[1, m], gx_r.at[1, m], (gid(xat(m), zh, c), r))
        put(ref, ref, gc_s.at[1, 0], gc_r.at[1, 0], (sib, r))

    def take_rows(half):
        def go():
            for m in range(4):
                arrived(rows_from(half, m, 1 - c), gc_s.at[half, m], gc_r.at[half, m], (sib, r))
            for xx in range(4):
                rows = pl.ds((4 * half + xx) * 2 * ROWS, 2 * ROWS)
                pair = rows_all[pl.ds(gid(xx, zh if half == 0 else 1 - zh, 0), 2)]
                th[rows], tl[rows] = split(pair.reshape(2 * ROWS, W))
        return go

    half_rows = W // 2
    halves = [pl.ds(i * half_rows, half_rows) for i in range(2)]

    def rows_dot(a, b):
        return lax.dot_general(a, b, (((0,), (0,)), ((), ())), preferred_element_type=F32)

    def gram_of(half, i):
        some, rows = halves[half], halves[i]
        gram = rows_dot(th[some, rows], th[some]) + rows_dot(th[some, rows], tl[some])
        return gram + rows_dot(tl[some, rows], th[some])

    def near_gram(i):
        def go():
            shifted[halves[i]] = gram_of(0, i)
        return go

    def statistic(i):
        def go():
            rows = halves[i]
            gram = shifted[rows] + gram_of(1, i)
            if i == 0:
                stat_copy.wait()
            stat_new = DECAY * stat_v[rows] + (1.0 - DECAY) * gram
            stat_out[0, rows] = stat_new
            count = step[0]
            power = jnp.float32(1.0)
            for n in range(12):
                power = jnp.where(n < count, power * DECAY, power)
            correction = 1.0 / (1.0 - jnp.full((8, 128), power, F32))
            shifted[rows] = stat_new * correction[0:1, 0:1] + jnp.where(eye_block(i * half_rows, half_rows), EPS, 0.0)
        return go

    def frobenius():
        value = shifted[...]
        return jnp.sqrt(jnp.sum(jnp.sum(value * value, axis=1, keepdims=True), axis=0, keepdims=True))

    def factor_from(i, coupled, high, low, keep_coupled=True):
        rows = halves[i]
        if keep_coupled:
            mh[rows], ml[rows] = split(coupled)
        high[rows], low[rows] = split((jnp.where(eye_block(i * half_rows, half_rows), 5.0, 0.0) - coupled) * 0.25)

    norm_of = []

    def start_newton():
        norm_of.append(frobenius())
        for i in range(2):
            factor_from(i, shifted[halves[i]] / norm_of[0], xh, xl)

    def product(a_high, a_low, b_high, b_low, give):
        def piece(i):
            def go():
                rows = halves[i]
                out = jnp.dot(a_high[rows], b_high[...], preferred_element_type=F32)
                out += jnp.dot(a_high[rows], b_low[...], preferred_element_type=F32)
                out += jnp.dot(a_low[rows], b_high[...], preferred_element_type=F32)
                give(i, rows, out)
            return go
        return [piece(0), piece(1)]

    def keep(high_ref, low_ref):
        def give(i, rows, out):
            high_ref[rows], low_ref[rows] = split(out)
        return give

    def couple(i, rows, out):
        shifted[rows] = out

    def next_factor(keep_coupled):
        def go():
            for i in range(2):
                factor_from(i, shifted[halves[i]], th, tl, keep_coupled)
        return go

    def finish(i, rows, out):
        root_out[0, rows] = (out / jnp.sqrt(jnp.sqrt(norm_of[0]))).astype(BF16)

    work = [take_rows(1), statistic(0), statistic(1), start_newton]
    work += product(xh, xl, xh, xl, keep(qh, ql)) + product(qh, ql, qh, ql, keep(th, tl))
    work += product(th, tl, mh, ml, couple) + [next_factor(True)]
    work += product(xh, xl, th, tl, keep(qh, ql)) + product(th, tl, th, tl, keep(xh, xl))
    work += product(xh, xl, xh, xl, keep(th, tl)) + product(th, tl, mh, ml, couple) + [next_factor(False)]
    work += product(qh, ql, th, tl, finish)

    ends = [(way, k, reach(way, k)) for k in (3, 2, 4, 5, 1, 0) for way in range(2)]
    for place, (way, k, h) in enumerate(RING + tuple(ends)):
        if place == AT_ACROSS:
            across(0)()
        if place == AT_NEAR:
            take_rows(0)()
        if place in (AT_NEAR + 1, AT_NEAR + 2):
            near_gram(place - AT_NEAR - 1)()
        if place == AT_FAR:
            far_rows()
        if place == AT_ACROSS_FAR:
            across(1)()
        if place >= AT_WORK and work:
            work.pop(0)()
        hop(way, k, h)
    for piece in work:
        piece()

    for copy in started:
        copy.wait_send()


def place_kernel(order, slots, stat, root, update, stat_out, root_out, sems):
    def update_copy(j):
        return pltpu.make_async_copy(slots.at[j], update.at[order[j]], sems.at[j])

    others = [
        pltpu.make_async_copy(stat, stat_out, sems.at[NB]),
        pltpu.make_async_copy(root, root_out, sems.at[NB + 1]),
    ]
    for copy in others:
        copy.start()
    for j in range(NB):
        update_copy(j).start()
    for copy in others:
        copy.wait()
    for j in range(NB):
        update_copy(j).wait()


def local(grad_parts, owner_order, step_count, stat_old, root_old):
    smem = pl.BlockSpec(memory_space=pltpu.SMEM)
    vmem = pl.BlockSpec(memory_space=pltpu.VMEM)
    hbm = pl.BlockSpec(memory_space=pltpu.HBM)
    sem = pltpu.SemaphoreType.DMA
    square = pltpu.VMEM((W, W), BF16)
    shapes = (
        jax.ShapeDtypeStruct((NB, ROWS, W), BF16),
        jax.ShapeDtypeStruct((1, W, W), F32),
        jax.ShapeDtypeStruct((1, W, W), BF16),
    )
    slots, stat_new, root_new = pl.pallas_call(
        kernel,
        out_shape=shapes,
        in_specs=[smem, hbm, hbm, hbm, hbm],
        out_specs=(vmem, vmem, vmem),
        scratch_shapes=[
            pltpu.SMEM((NB,), jnp.int32),
            pltpu.VMEM((NB, ROWS, W), BF16),
            pltpu.VMEM((2, NZ, ROWS, CA), BF16),
            pltpu.VMEM((2, NZ, ROWS, CA), BF16),
            pltpu.VMEM((2, NZ, 3, ROWS, CA), F32),
            pltpu.VMEM((2, NZ, 3, ROWS, CA), F32),
            pltpu.VMEM((NZ - 1, NY, ROWS, W - CA), BF16),
            pltpu.VMEM((NZ, NY, ROWS, W - CA), BF16),
            pltpu.VMEM((NY, ROWS, W - CA), F32),
            pltpu.VMEM((NY - 1, ROWS, W - CA), F32),
            pltpu.VMEM((NZ - 1, ROWS, CA), F32),
            pltpu.VMEM((NZ, ROWS, CA), F32),
            pltpu.VMEM((ROWS, W), F32),
            pltpu.VMEM((1, 128), F32),
            pltpu.VMEM((15, 1, 128), F32),
            pltpu.VMEM((16, ROWS, W), F32),
            pltpu.VMEM((W, W), F32),
            pltpu.VMEM((W, W), BF16),
            square, square, square, square, square, square, square, square,
            pltpu.VMEM((W, W), F32),
            sem((2, NZ, 4)), sem((2, NZ, 4)),
            sem((NZ - 1,)), sem((NZ,)),
            sem((NY - 1,)), sem((NY - 1,)),
            sem((NZ - 1,)), sem((NZ,)),
            sem((15,)), sem((15,)),
            sem((2, 4)), sem((2, 4)),
            sem((2, 4)), sem((2, 4)),
            sem, sem,
            sem((NZ - 1,)), sem((NZ,)),
            sem((2, NZ, 4)), sem((2, NZ, 4)),
            sem((4,)),
        ],
        compiler_params=pltpu.CompilerParams(
            collective_id=0, has_side_effects=True, vmem_limit_bytes=48 * 2**20
        ),
        name="shampoo_step",
    )(step_count, *(pltpu.with_memory_space_constraint(a, pltpu.HBM) for a in (owner_order, grad_parts, stat_old, root_old)))
    return pl.pallas_call(
        place_kernel,
        out_shape=shapes,
        in_specs=[smem, vmem, vmem, vmem],
        out_specs=(hbm, hbm, hbm),
        scratch_shapes=[sem((NB + 2,))],
        compiler_params=pltpu.CompilerParams(vmem_limit_bytes=8 * 2**20),
        name="place",
    )(owner_order, slots, stat_new, root_new)


def solution(mesh):
    placed = (
        P("replica", None, "group", None),
        P(),
        P(),
        P("replica", None, None),
        P("replica", None, None),
    )
    return jax.shard_map(
        local,
        mesh=mesh,
        in_specs=placed,
        out_specs=(P(None, "group", None), P("replica", None, None), P("replica", None, None)),
        check_vma=False,
    )
```
